256 devices in a mesh: row: 8 (over x, core), col: 32 (over y, z).
Axes of the slice: x: 4, y: 4, z: 8, core: 2. Of those that a mesh axis runs over, the one named last changes fastest.
Arguments:
- features: bfloat16 [65536, 512], P('col', 'row'), may hold values from -6 to 6
- weight: bfloat16 [512, 512], replicated, may hold values from -0.25 to 0.25
- bias: float32 [512], replicated, may hold values from -3 to 3
- edge_src: int32 [512, 16384], P('row', 'col'), may hold values from 0 to 2047
- edge_dst: int32 [512, 16384], P('row', 'col'), may hold values from 0 to 127
- tile_count: int32 [512, 32], P('row', 'col'), may hold values from 0 to 512, as said below
Outputs:
- layer_out: bfloat16 [65536, 512], P(('row', 'col'))
The draws below stay inside these ranges and needn't reach their ends.
Inputs may be any that keep to these rules, and one draw needn't show every extreme that they name: `tile_count`: entries of a tile past its count are padding and carry no edge. Some tile holds exactly 512 live edges from one sending block in every draw.
All inputs are finite; a program needn't handle non-finite values.
Results may differ from the reference program's by a relative error of at most 0.0034.
Values may be sent and summed in bfloat16 or wider, within the bound.
A program may use at most 128 MiB of HBM per device.

```python
import math
import jax
import jax.numpy as jnp
import numpy as np
from jax import lax

F = 512
TILE = 128
EDGE_CAP = 512
NODES = 65536
TILES = 512
BLOCK_ROWS = 8192
SRC_ROWS = 2048
N_COL = 32


def draw_tile_count(key, part):
    column_count = NODES // SRC_ROWS
    row_count = NODES // BLOCK_ROWS
    key_one, key_two, key_three = jax.random.split(key, 3)
    tile_index = jnp.arange(TILES, dtype=jnp.int32)[:, None]
    column = jnp.arange(column_count, dtype=jnp.int32)[None, :]
    row_block = tile_index // (TILES // row_count)
    limit_cap = EDGE_CAP * (row_count - 1 + 2 * row_block) * (column_count - 1 + 2 * column) // (9 * (row_count - 1) * (column_count - 1))
    limit_cap = jnp.maximum(limit_cap, 1)
    first_draw = jax.random.randint(key_one, (TILES, column_count), 0, EDGE_CAP + 1)
    second_draw = jax.random.randint(key_two, (TILES, column_count), 0, EDGE_CAP + 1)
    reduction = limit_cap * (first_draw * second_draw // (EDGE_CAP + 1)) // (EDGE_CAP + 1)
    counts = limit_cap - reduction
    chosen = jax.random.randint(key_three, (), TILES - TILES // row_count, TILES)
    full_slot = (tile_index == chosen) & (column == column_count - 1)
    return jnp.where(full_slot, EDGE_CAP, counts).astype(jnp.int32)


def set_ends(result, stream_key, low, top_value):
    longest = result.shape.index(max(result.shape))
    spots = []
    for shift in (0, 1):
        where = [jax.random.randint(jax.random.fold_in(stream_key, axis), (), 0, length) for axis, length in enumerate(result.shape)]
        where[longest] = (where[longest] + shift) % result.shape[longest]
        spots.append(tuple(where))
    return result.at[spots[0]].set(low).at[spots[1]].set(top_value)


def block_levels(key, shape, pieces, low, largest):
    loudness = 1.0
    for axis_at, blocks in pieces:
        steps = jax.random.uniform(jax.random.fold_in(jax.random.fold_in(key, 6), axis_at), (blocks,), jnp.float32, low / len(pieces), largest / len(pieces))
        loudness = loudness * jnp.repeat(jnp.exp(steps), shape[axis_at] // blocks).reshape((-1,) + (1,) * (len(shape) - 1 - axis_at))
    return loudness


def cumulative_ranks(number_of, skew):
    loads = [(1 << 20) // math.isqrt(rank ** skew) + 1 for rank in range(1, number_of + 1)]
    scale = 1 + sum(loads) // (1 << 30)
    return np.cumsum(np.array([max(1, weight // scale) for weight in loads]))


def ranked_ids(stream_key, dims, number_of, skew):
    listing = cumulative_ranks(number_of, skew)
    pick = jax.random.randint(jax.random.fold_in(stream_key, 1), dims, 0, int(listing[number_of - 1]))
    grade = jnp.searchsorted(jnp.asarray(listing, jnp.int32), pick, side="right")
    return jax.random.permutation(jax.random.fold_in(stream_key, 2), number_of)[grade].astype(jnp.int32)


def centred(key, extent, spread, limit, cuts=(), held_as=jnp.bfloat16):
    level = block_levels(key, extent, cuts, -0.22, 0.18) if cuts else 1.0
    values = jax.random.normal(key, extent, jnp.float32) * spread * level
    return jnp.minimum(jnp.maximum(values, -limit), limit).astype(held_as)


def setup_inputs(seed: int = 0) -> dict:
    keys = jax.random.split(jax.random.key(seed), 7)
    return {
        "features": centred(keys[0], (NODES, F), 1.0, 6.0, ((0, 32), (1, 8))),
        "weight": centred(keys[1], (F, F), F ** -0.5, 0.25),
        "bias": centred(keys[2], (F,), 0.5, 3.0, (), jnp.float32),
        "edge_src": set_ends(ranked_ids(keys[3], (TILES, N_COL * EDGE_CAP), SRC_ROWS, 2), jax.random.fold_in(keys[3], 3), 0, SRC_ROWS - 1).astype(jnp.int32),
        "edge_dst": set_ends(jax.random.randint(keys[4], (TILES, N_COL * EDGE_CAP), 0, TILE), jax.random.fold_in(keys[4], 1), 0, TILE - 1).astype(jnp.int32),
        "tile_count": draw_tile_count(jax.random.fold_in(keys[6], 71), 0),
    }


def reference(features, weight, bias, edge_src, edge_dst, tile_count):
    node_total, feat_width = features.shape
    tile_total, slot_total = edge_src.shape
    block_count = tile_count.shape[1]
    slot_cap = slot_total // block_count
    slot_index = jnp.arange(slot_total, dtype=jnp.int32)
    block_of = slot_index // slot_cap
    within = slot_index - block_of * slot_cap
    limits = jnp.repeat(tile_count, slot_cap, axis=1)
    live_mask = (within[None, :] < limits).astype(jnp.float32)
    source_all = block_of[None, :] * (node_total // block_count) + edge_src
    tile_base = jnp.arange(tile_total, dtype=jnp.int32)[:, None] * TILE
    target_all = tile_base + edge_dst
    out_degree = jnp.zeros((node_total,), jnp.float32).at[source_all.reshape(-1)].add(live_mask.reshape(-1))
    in_degree = jnp.zeros((node_total,), jnp.float32).at[target_all.reshape(-1)].add(live_mask.reshape(-1))
    scaled = (features.astype(jnp.float32) * lax.rsqrt(1.0 + out_degree)[:, None]).astype(jnp.bfloat16)

    def one_tile(packed):
        source, target, weights = packed
        values = scaled[source].astype(jnp.float32) * weights[:, None]
        return jnp.zeros((TILE, feat_width), jnp.float32).at[target].add(values)
    aggregate = lax.map(one_tile, (source_all, edge_dst, live_mask)).reshape(node_total, feat_width)
    normed = (aggregate * lax.rsqrt(1.0 + in_degree)[:, None]).astype(jnp.bfloat16)
    projected = jnp.dot(normed, weight, preferred_element_type=jnp.float32) + bias
    return jax.nn.relu(projected).astype(jnp.bfloat16)
```

```python
import functools

import jax
import jax.numpy as jnp
from jax import lax
from jax.experimental import pallas as pl
from jax.experimental.pallas import tpu as pltpu
from jax.sharding import PartitionSpec as P

TILE = 128
F = 512
SRC = 2048
CAP = 512
TILES = 64
NROW = 8
NY = 4
NZ = 8
AHEAD = 3
bf16 = jnp.bfloat16
f32 = jnp.float32
f8 = jnp.float8_e4m3fn
MESH = pl.DeviceIdType.MESH
NT = (((1,), (1,)), ((), ()))


def onehot(row, size):
    parts = []
    for base in range(0, size, 256):
        width = min(256, size - base)
        value = (row - base).astype(f32).astype(bf16)
        places = lax.broadcasted_iota(jnp.int32, (width, row.shape[1]), 0).astype(f32).astype(bf16)
        parts.append(jnp.where(places == value, jnp.ones((), bf16), jnp.zeros((), bf16)).astype(f8))
    return parts[0] if len(parts) == 1 else jnp.concatenate(parts, axis=0)


def kernel(
    xt, src, dst, cnt, weight, bias, out,
    xg, xs, deg, deg_in, cin, cin_in, cmid, cmid_in, amat,
    zs, zr, ys, yr, p1, p1_in, p2, p2_in, acc_z, acc_y,
    x_sem, d_sem, c_sem, m_sem, z_sem, y_sem, p1_sem, p2_sem, own_sem,
):
    r = lax.axis_index("row")
    c = lax.axis_index("col")
    y = c // NZ
    z = lax.rem(c, NZ)

    def row_peer(k):
        return (lax.rem(r + k, NROW), c)

    def z_peer(k):
        return (r, y * NZ + lax.rem(z + k, NZ))

    def y_peer(k):
        return (r, lax.rem(y + k, NY) * NZ + z)

    barrier = pltpu.get_barrier_semaphore()
    peers = [row_peer(k) for k in range(1, NROW)]
    peers += [z_peer(k) for k in range(1, NZ)]
    peers += [y_peer(k) for k in range(1, NY)]
    for peer in peers:
        pl.semaphore_signal(barrier, inc=1, device_id=peer, device_id_type=MESH)
    pl.semaphore_wait(barrier, len(peers))

    def remote(source, target, sems, index, peer):
        return pltpu.make_async_remote_copy(
            src_ref=source, dst_ref=target, send_sem=sems.at[(0,) + index],
            recv_sem=sems.at[(1,) + index], device_id=peer, device_id_type=MESH,
        )

    x_copies = [remote(xt, xg.at[r], x_sem, (k - 1,), row_peer(k)) for k in range(1, NROW)]
    for copy in x_copies:
        copy.start()
    own = pltpu.make_async_copy(xt, xg.at[r], own_sem)
    own.start()

    slots = lax.broadcasted_iota(jnp.int32, (1, CAP), 1)

    def edges(t):
        return src[pl.ds(t, 1), :], dst[pl.ds(t, 1), :], slots < cnt[0, t]

    def count_step(zi, total):
        rows = []
        for j in range(8):
            s, d, valid = edges(2 * ((j // 2) * NZ + zi) + j % 2)
            left = jnp.concatenate(
                [onehot(jnp.where(valid, s >> 7, -1), 32), jnp.ones((32, CAP), f8)], axis=0
            )
            right = jnp.concatenate(
                [onehot(s & 127, 128), onehot(jnp.where(valid, d, -1), 128)], axis=0
            )
            both = lax.dot_general(left, right, NT, preferred_element_type=f32)
            total = total + both[:16, :128]
            rows.append(both[32:33, 128:])
        cin[zi] = jnp.concatenate(rows, axis=0)
        return total

    deg[...] = lax.fori_loop(0, NZ, count_step, jnp.zeros((16, 128), f32))
    d_copies = [remote(deg, deg_in.at[k - 1], d_sem, (k - 1,), row_peer(k)) for k in range(1, NROW)]
    for copy in d_copies:
        copy.start()
    c_copies = [
        remote(cin.at[lax.rem(z + k, NZ)], cin_in.at[k - 1], c_sem, (k - 1,), z_peer(k))
        for k in range(1, NZ)
    ]
    for copy in c_copies:
        copy.start()

    def build(t, slot):
        s, d, valid = edges(t)
        place = jnp.where(valid, (s >> 9) * TILE + d, -1)
        count = lax.dot_general(
            onehot(place, 512), onehot(s & 511, 512), NT, preferred_element_type=f32
        )
        base = pl.multiple_of(slot * TILE, TILE)
        for h in range(4):
            amat[pl.ds(base, TILE), h * 512 : (h + 1) * 512] = count[
                h * TILE : (h + 1) * TILE
            ].astype(bf16)

    def build_z(step):
        def one(j, carry):
            for u in range(2):
                jj = 2 * u + j
                zi = lax.rem(z + NZ - 1 - step, NZ) if u == 0 else lax.rem(z + 1 + step, NZ)
                build(2 * (jj * NZ + zi), step * 4 + jj)
            return carry

        lax.fori_loop(0, 2, one, 0)

    def build_y(step):
        def one(j, carry):
            for u in range(2):
                jj = 4 * u + j
                yi = lax.rem(y + NY - 1 - step, NY) if u == 0 else lax.rem(y + 1 + step, NY)
                build(2 * (yi * NZ + jj) + 1, 32 + step * 8 + jj)
            return carry

        lax.fori_loop(0, 4, one, 0)

    def build_step(step):
        build_z(step)

        @pl.when(lax.rem(step, 2) == 0)
        def _():
            build_y(step // 2)

    def ahead(step, carry):
        build_step(step)
        return carry

    lax.fori_loop(0, AHEAD, ahead, 0)

    for copy in d_copies:
        copy.wait()
    total = deg[...]
    for k in range(1, NROW):
        total = total + deg_in[k - 1]
    scale = lax.rsqrt(1.0 + total)
    for copy in c_copies:
        copy.wait()
    mid = cin[z]
    for k in range(1, NZ):
        mid = mid + cin_in[k - 1]
    cmid[...] = mid
    m_copies = [remote(cmid, cmid_in.at[k - 1], m_sem, (k - 1,), y_peer(k)) for k in range(1, NY)]
    for copy in m_copies:
        copy.start()
    for copy in x_copies:
        copy.wait()
    own.wait()

    def scale_rows(i, carry):
        base = pl.multiple_of(i * 64, 64)
        for h in range(16):
            cols = slice(h * 128, (h + 1) * 128)
            xs[pl.ds(base, 64), cols] = (xg[i, :, cols].astype(f32) * scale[h : h + 1, :]).astype(bf16)
        return carry

    lax.fori_loop(0, NROW, scale_rows, 0)

    def z_copy(d, s):
        return remote(zs.at[d, s], zr.at[d, s], z_sem, (d, s), z_peer(1 if d == 0 else NZ - 1))

    def y_copy(d, s):
        return remote(ys.at[d, s], yr.at[d, s], y_sem, (d, s), y_peer(1 if d == 0 else NY - 1))

    def product(slot, tiles):
        base = pl.multiple_of(slot * TILE, TILE)
        return lax.dot_general(
            amat[pl.ds(base, tiles * TILE), :], xs[...], NT, preferred_element_type=f32
        )

    p2_copies = [
        remote(p2.at[lax.rem(z + k, NZ)], p2_in.at[k - 1], p2_sem, (k - 1,), z_peer(k))
        for k in range(1, NZ)
    ]
    p1_copies = [
        remote(p1.at[lax.rem(y + k, NY)], p1_in.at[k - 1], p1_sem, (k - 1,), y_peer(k))
        for k in range(1, NY)
    ]

    def ring_step(step, carry):
        for d in range(2):
            acc_z[...] = product(step * 4 + 2 * d, 2)

            @pl.when(step > 0)
            def _():
                z_copy(d, step - 1).wait_recv()
                acc_z[...] += zr[d, step - 1].astype(f32)

            @pl.when(step < NZ - 1)
            def _():
                zs[d, step] = acc_z[...].astype(bf16)
                z_copy(d, step).start()

            @pl.when(step == NZ - 1)
            def _():
                for u in range(2):
                    p1[2 * d + u] = acc_z[u * TILE : (u + 1) * TILE].astype(bf16)

        @pl.when(lax.rem(step, 2) == 0)
        def _():
            q = step // 2
            for d in range(2):
                acc_y[...] = product(32 + q * 8 + 4 * d, 4)

                @pl.when(q > 0)
                def _():
                    y_copy(d, q - 1).wait_recv()
                    acc_y[...] += yr[d, q - 1].astype(f32)

                @pl.when(q < NY - 1)
                def _():
                    ys[d, q] = acc_y[...].astype(bf16)
                    y_copy(d, q).start()

                @pl.when(q == NY - 1)
                def _():
                    for u in range(4):
                        p2[4 * d + u] = acc_y[u * TILE : (u + 1) * TILE].astype(bf16)

            @pl.when(q == NY - 1)
            def _():
                for copy in p2_copies:
                    copy.start()

        @pl.when(step + AHEAD < NZ)
        def _():
            build_step(step + AHEAD)

        return carry

    lax.fori_loop(0, NZ, ring_step, 0)
    for copy in p1_copies:
        copy.start()

    for copy in m_copies:
        copy.wait()
    degree = cmid[pl.ds(2 * y, 2), :]
    for k in range(1, NY):
        degree = degree + cmid_in[k - 1, pl.ds(2 * y, 2), :]
    norm = jnp.transpose(lax.rsqrt(1.0 + jnp.concatenate([degree] * 4, axis=0)))

    def finish(half, total):
        normed = (total * norm[:, half : half + 1]).astype(bf16)
        result = jnp.dot(normed, weight[...], preferred_element_type=f32) + bias[...]
        out[half * TILE : (half + 1) * TILE, :] = jnp.maximum(result, 0.0).astype(bf16)

    for copy in p1_copies:
        copy.wait()
    total = p1[y].astype(f32)
    for k in range(1, NY):
        total = total + p1_in[k - 1].astype(f32)
    finish(0, total)
    for copy in p2_copies:
        copy.wait()
    total = p2[z].astype(f32)
    for k in range(1, NZ):
        total = total + p2_in[k - 1].astype(f32)
    finish(1, total)

    def drain(step, carry):
        for d in range(2):
            z_copy(d, step).wait_send()
        return carry

    lax.fori_loop(0, NZ - 1, drain, 0)

    def drain_y(step, carry):
        for d in range(2):
            y_copy(d, step).wait_send()
        return carry

    lax.fori_loop(0, NY - 1, drain_y, 0)


def body(features, weight, bias, edge_src, edge_dst, tile_count):
    vmem = pl.BlockSpec(memory_space=pltpu.VMEM)
    smem = pl.BlockSpec(memory_space=pltpu.SMEM)
    units = features.shape[1]
    dma = pltpu.SemaphoreType.DMA
    return pl.pallas_call(
        kernel,
        out_shape=jax.ShapeDtypeStruct((2 * TILE, F), bf16),
        in_specs=[vmem, vmem, vmem, smem, vmem, vmem],
        out_specs=vmem,
        scratch_shapes=[
            pltpu.VMEM((NROW, units, SRC), bf16),
            pltpu.VMEM((F, SRC), bf16),
            pltpu.VMEM((16, 128), f32),
            pltpu.VMEM((NROW - 1, 16, 128), f32),
            pltpu.VMEM((NZ, 8, 128), f32),
            pltpu.VMEM((NZ - 1, 8, 128), f32),
            pltpu.VMEM((8, 128), f32),
            pltpu.VMEM((NY - 1, 8, 128), f32),
            pltpu.VMEM((TILES * TILE, SRC), bf16),
            pltpu.VMEM((2, NZ - 1, 2 * TILE, F), bf16),
            pltpu.VMEM((2, NZ - 1, 2 * TILE, F), bf16),
            pltpu.VMEM((2, NY - 1, 4 * TILE, F), bf16),
            pltpu.VMEM((2, NY - 1, 4 * TILE, F), bf16),
            pltpu.VMEM((NY, TILE, F), bf16),
            pltpu.VMEM((NY - 1, TILE, F), bf16),
            pltpu.VMEM((NZ, TILE, F), bf16),
            pltpu.VMEM((NZ - 1, TILE, F), bf16),
            pltpu.VMEM((2 * TILE, F), f32),
            pltpu.VMEM((4 * TILE, F), f32),
            dma((2, NROW - 1)),
            dma((2, NROW - 1)),
            dma((2, NZ - 1)),
            dma((2, NY - 1)),
            dma((2, 2, NZ - 1)),
            dma((2, 2, NY - 1)),
            dma((2, NY - 1)),
            dma((2, NZ - 1)),
            dma,
        ],
        compiler_params=pltpu.CompilerParams(
            collective_id=0, has_side_effects=True, vmem_limit_bytes=60 * 1024 * 1024
        ),
        name="graph_layer",
    )(features.T, edge_src, edge_dst, tile_count.T, weight, bias[None, :])


def solution(mesh):
    in_specs = (P("col", "row"), P(), P(), P("row", "col"), P("row", "col"), P("row", "col"))
    out_specs = P(("row", "col"), None)
    return jax.shard_map(body, mesh=mesh, in_specs=in_specs, out_specs=out_specs, check_vma=False)
```

```python
import functools

import jax
import jax.numpy as jnp
from jax import lax
from jax.experimental import pallas as pl
from jax.experimental.pallas import tpu as pltpu
from jax.sharding import PartitionSpec as P

TILE = 128
F = 512
SRC = 2048
CAP = 512
TILES = 64
NROW = 8
NY = 4
NZ = 8
AHEAD = 2
HALF = 64
STEP = 1024
bf16 = jnp.bfloat16
f32 = jnp.float32
f8 = jnp.float8_e4m3fn
MESH = pl.DeviceIdType.MESH
NT = (((1,), (1,)), ((), ()))


def onehot(row, size):
    parts = []
    for base in range(0, size, 256):
        width = min(256, size - base)
        value = (row - base).astype(f32).astype(bf16)
        places = lax.broadcasted_iota(jnp.int32, (width, row.shape[1]), 0).astype(f32).astype(bf16)
        parts.append(jnp.where(places == value, jnp.ones((), bf16), jnp.zeros((), bf16)).astype(f8))
    return parts[0] if len(parts) == 1 else jnp.concatenate(parts, axis=0)


def kernel(
    xt, src, dst, cnt, weight, bias, out,
    xg, xs, deg, deg_in, cin, cin_in, cmid, cmid_in, amat,
    zs, zr, ys, yr, p1, p1_in, p2, p2_out, p2_in, acc,
    x_sem, d_sem, c_sem, m_sem, z_sem, y_sem, p1_sem, p2_sem, own_sem,
):
    r = lax.axis_index("row")
    c = lax.axis_index("col")
    y = c // NZ
    z = lax.rem(c, NZ)

    def row_peer(k):
        return (lax.rem(r + k, NROW), c)

    def z_peer(k):
        return (r, y * NZ + lax.rem(z + k, NZ))

    def y_peer(k):
        return (r, lax.rem(y + k, NY) * NZ + z)

    barrier = pltpu.get_barrier_semaphore()
    peers = [row_peer(k) for k in range(1, NROW)]
    peers += [z_peer(k) for k in range(1, NZ)]
    peers += [y_peer(k) for k in range(1, NY)]
    for peer in peers:
        pl.semaphore_signal(barrier, inc=1, device_id=peer, device_id_type=MESH)
    pl.semaphore_wait(barrier, len(peers))

    def remote(source, target, sems, index, peer):
        return pltpu.make_async_remote_copy(
            src_ref=source, dst_ref=target, send_sem=sems.at[(0,) + index],
            recv_sem=sems.at[(1,) + index], device_id=peer, device_id_type=MESH,
        )

    after, before, opposite = (lax.rem(r + k, NROW) for k in (2, 6, 4))
    sibling = (r + 1 - 2 * lax.rem(r, 2), c)
    low, high = pl.ds(0, 32), pl.ds(32, 32)

    def x_copy(index, source, target, peer):
        return remote(source, target, x_sem, (index,), peer)

    right_low = x_copy(0, xt.at[low], xg.at[r, low], (after, c))
    left_high = x_copy(1, xt.at[high], xg.at[r, high], (before, c))
    right_high = x_copy(2, xt.at[high], xg.at[r, high], (after, c))
    left_low = x_copy(3, xt.at[low], xg.at[r, low], (before, c))
    own_across = x_copy(4, xt, xg.at[r], sibling)
    on_right = x_copy(5, xg.at[before, low], xg.at[before, low], (after, c))
    on_left = x_copy(6, xg.at[after, high], xg.at[after, high], (before, c))
    before_across = x_copy(7, xg.at[before], xg.at[before], sibling)
    after_across = x_copy(8, xg.at[after], xg.at[after], sibling)
    opposite_across = x_copy(9, xg.at[opposite], xg.at[opposite], sibling)
    for copy in (right_low, left_high, right_high, left_low, own_across):
        copy.start()
    own = pltpu.make_async_copy(xt, xg.at[r], own_sem)
    own.start()

    slots = lax.broadcasted_iota(jnp.int32, (1, CAP), 1)

    def edges(t):
        return src[pl.ds(t, 1), :], dst[pl.ds(t, 1), :], slots < cnt[0, t]

    def count_step(zi, total):
        rows = []
        for j in range(8):
            s, d, valid = edges(2 * ((j // 2) * NZ + zi) + j % 2)
            left = jnp.concatenate(
                [onehot(jnp.where(valid, s >> 7, -1), 32), jnp.ones((32, CAP), f8)], axis=0
            )
            right = jnp.concatenate(
                [onehot(s & 127, 128), onehot(jnp.where(valid, d, -1), 128)], axis=0
            )
            both = lax.dot_general(left, right, NT, preferred_element_type=f32)
            total = total + both[:16, :128]
            rows.append(both[32:33, 128:])
        cin[zi] = jnp.concatenate(rows, axis=0)
        return total

    deg[...] = lax.fori_loop(0, NZ // 2, count_step, jnp.zeros((16, 128), f32))
    right_low.wait_recv()
    on_right.start()
    left_high.wait_recv()
    on_left.start()
    deg[...] = lax.fori_loop(NZ // 2, NZ, count_step, deg[...])
    d_copies = [remote(deg, deg_in.at[k - 1], d_sem, (k - 1,), row_peer(k)) for k in range(1, NROW)]
    for copy in d_copies:
        copy.start()
    c_copies = [
        remote(cin.at[lax.rem(z + k, NZ)], cin_in.at[k - 1], c_sem, (k - 1,), z_peer(k))
        for k in range(1, NZ)
    ]
    for copy in c_copies:
        copy.start()
    right_high.wait_recv()
    before_across.start()
    left_low.wait_recv()
    after_across.start()

    def count_matrix(t):
        s, d, valid = edges(t)
        place = jnp.where(valid, (s >> 9) * TILE + d, -1)
        return lax.dot_general(
            onehot(place, 512), onehot(s & 511, 512), NT, preferred_element_type=f32
        ).astype(bf16)

    def build_z(step):
        def one(j, carry):
            for u in range(2):
                jj = 2 * u + j
                zi = lax.rem(z + NZ - 1 - step, NZ) if u == 0 else lax.rem(z + 1 + step, NZ)
                count = count_matrix(2 * (jj * NZ + zi))
                base = pl.multiple_of(step * STEP + jj * TILE, TILE)
                for h in range(4):
                    amat[pl.ds(base, TILE), h * 512 : (h + 1) * 512] = count[
                        h * TILE : (h + 1) * TILE
                    ]
            return carry

        lax.fori_loop(0, 2, one, 0)

    def build_y(group):
        q = group // 2
        d = lax.rem(group, 2)
        yi = lax.rem(y + 2 * NY + (2 * d - 1) * (q + 1), NY)

        def one(j, carry):
            for u in range(2):
                jj = 2 * j + u
                count = count_matrix(2 * (yi * NZ + 4 * d + jj) + 1)
                for part in range(2):
                    base = pl.multiple_of((2 * q + part) * STEP + 512 + d * 256 + jj * HALF, HALF)
                    for h in range(4):
                        start = h * TILE + part * HALF
                        amat[pl.ds(base, HALF), h * 512 : (h + 1) * 512] = count[
                            start : start + HALF
                        ]
            return carry

        lax.fori_loop(0, 2, one, 0)

    def ahead(step, carry):
        build_z(step)
        build_y(step + 1)
        return carry

    build_y(0)
    lax.fori_loop(0, AHEAD - 1, ahead, 0)
    on_right.wait_recv()
    on_left.wait_recv()
    opposite_across.start()
    lax.fori_loop(AHEAD - 1, AHEAD, ahead, 0)

    for copy in d_copies:
        copy.wait()
    total = deg[...]
    for k in range(1, NROW):
        total = total + deg_in[k - 1]
    scale = lax.rsqrt(1.0 + total)
    for copy in c_copies:
        copy.wait()
    mid = cin[z]
    for k in range(1, NZ):
        mid = mid + cin_in[k - 1]
    cmid[...] = mid
    m_copies = [remote(cmid, cmid_in.at[k - 1], m_sem, (k - 1,), y_peer(k)) for k in range(1, NY)]
    for copy in m_copies:
        copy.start()
    for copy in (own_across, before_across, after_across, opposite_across):
        copy.wait_recv()
    own.wait()

    def scale_rows(i, carry):
        base = pl.multiple_of(i * 64, 64)
        for h in range(16):
            cols = slice(h * 128, (h + 1) * 128)
            xs[pl.ds(base, 64), cols] = (xg[i, :, cols].astype(f32) * scale[h : h + 1, :]).astype(bf16)
        return carry

    lax.fori_loop(0, NROW, scale_rows, 0)

    def product(step):
        def one(i, carry):
            base = pl.multiple_of(step * STEP + i * 512, 512)
            acc[pl.ds(pl.multiple_of(i * 512, 512), 512), :] = lax.dot_general(
                amat[pl.ds(base, 512), :], xs[...], NT, preferred_element_type=f32
            )
            return carry

        lax.fori_loop(0, 2, one, 0)

    def z_copy(d, s, u):
        rows = pl.ds(u * TILE, TILE)
        return remote(
            zs.at[d, lax.rem(s, 2), rows], zr.at[d, s, rows], z_sem, (d, s, u),
            z_peer(1 if d == 0 else NZ - 1),
        )

    def y_copy(d, s):
        return remote(ys.at[d, s], yr.at[d, s], y_sem, (d, s), y_peer(1 if d == 0 else NY - 1))

    def z_add(d, s, u):
        z_copy(d, s - 1, u).wait_recv()
        rows = slice(d * 256 + u * TILE, d * 256 + (u + 1) * TILE)
        acc[rows] += zr[d, s - 1, u * TILE : (u + 1) * TILE].astype(f32)

    def z_part(d, s, u):
        @pl.when(s > 0)
        def _():
            z_add(d, s, u)

        @pl.when(s > 1)
        def _():
            z_copy(d, s - 2, u).wait_send()

        rows = slice(d * 256 + u * TILE, d * 256 + (u + 1) * TILE)
        zs[d, lax.rem(s, 2), u * TILE : (u + 1) * TILE] = acc[rows].astype(bf16)
        z_copy(d, s, u).start()

    def y_part(d, s):
        rows = slice(512 + d * 256, 768 + d * 256)

        @pl.when(s > 1)
        def _():
            y_copy(d, s - 2).wait_recv()
            acc[rows] += yr[d, s - 2].astype(f32)

        ys[d, s] = acc[rows].astype(bf16)
        y_copy(d, s).start()

    def y_last(part):
        for d in range(2):
            y_copy(d, 4 + part).wait_recv()
            for u in range(4):
                first = 512 + d * 256 + u * HALF
                p2[part, 4 * d + u] = acc[first : first + HALF] + yr[
                    d, 4 + part, u * HALF : (u + 1) * HALF
                ].astype(f32)

    def p2_copy(part, slot):
        return remote(
            p2_out.at[part, slot], p2_in.at[part, slot], p2_sem, (part, slot),
            z_peer(1 if slot < 4 else NZ - 1),
        )

    def p2_hop(part, hop):
        for slot in (hop, 4 + hop) if hop < 3 else (hop,):
            zi = lax.rem(z + (4 - hop if slot < 4 else 5 + hop), NZ)
            value = p2[part, zi]
            if hop > 0:
                p2_copy(part, slot - 1).wait_recv()
                value = value + p2_in[part, slot - 1].astype(f32)
            p2_out[part, slot] = value.astype(bf16)
            p2_copy(part, slot).start()

    def ring_step(s, carry):
        product(s)

        @pl.when(s + AHEAD < NZ)
        def _():
            build_z(s + AHEAD)

        @pl.when(s + AHEAD + 1 < NZ)
        def _():
            build_y(s + AHEAD + 1)

        for d in range(2):
            z_part(d, s, 0)

        @pl.when(s < 6)
        def _():
            for d in range(2):
                y_part(d, s)

        for d in range(2):
            z_part(d, s, 1)
        return carry

    lax.fori_loop(0, NZ - 1, ring_step, 0)
    y_last(0)
    p2_hop(0, 0)
    product(NZ - 1)
    p2_hop(0, 1)
    y_last(1)
    p2_hop(1, 0)
    p2_hop(0, 2)
    p1_copies = [
        remote(p1.at[lax.rem(y + k, NY)], p1_in.at[k - 1], p1_sem, (k - 1,), y_peer(k))
        for k in range(1, NY)
    ]
    for u in range(2):
        for d in range(2):
            z_add(d, NZ - 1, u)
            first = (2 * d + u) * TILE
            p1[2 * d + u] = acc[first : first + TILE].astype(bf16)
    for copy in p1_copies:
        copy.start()
    p2_hop(1, 1)
    p2_hop(0, 3)
    p2_hop(1, 2)
    p2_hop(1, 3)

    for copy in m_copies:
        copy.wait()
    degree = cmid[pl.ds(2 * y, 2), :]
    for k in range(1, NY):
        degree = degree + cmid_in[k - 1, pl.ds(2 * y, 2), :]
    norm = jnp.transpose(lax.rsqrt(1.0 + jnp.concatenate([degree] * 4, axis=0)))

    def finish(half, total):
        normed = (total * norm[:, half : half + 1]).astype(bf16)
        result = jnp.dot(normed, weight[...], preferred_element_type=f32) + bias[...]
        out[half * TILE : (half + 1) * TILE, :] = jnp.maximum(result, 0.0).astype(bf16)

    for copy in p1_copies:
        copy.wait()
    total = acc[pl.ds(pl.multiple_of(y * TILE, TILE), TILE), :]
    for k in range(1, NY):
        total = total + p1_in[k - 1].astype(f32)
    finish(0, total)
    totals = []
    for part in range(2):
        total = p2[part, z]
        for slot in (3, 6):
            p2_copy(part, slot).wait_recv()
            total = total + p2_in[part, slot].astype(f32)
        totals.append(total)
    finish(1, jnp.concatenate(totals, axis=0))

    for copy in (
        right_low, left_high, right_high, left_low, own_across,
        on_right, on_left, before_across, after_across, opposite_across,
    ):
        copy.wait_send()
    for d in range(2):
        for s in (NZ - 3, NZ - 2):
            for u in range(2):
                z_copy(d, s, u).wait_send()
        for s in range(6):
            y_copy(d, s).wait_send()
    for part in range(2):
        for slot in range(7):
            p2_copy(part, slot).wait_send()


def body(features, weight, bias, edge_src, edge_dst, tile_count):
    vmem = pl.BlockSpec(memory_space=pltpu.VMEM)
    smem = pl.BlockSpec(memory_space=pltpu.SMEM)
    units = features.shape[1]
    dma = pltpu.SemaphoreType.DMA
    return pl.pallas_call(
        kernel,
        out_shape=jax.ShapeDtypeStruct((2 * TILE, F), bf16),
        in_specs=[vmem, vmem, vmem, smem, vmem, vmem],
        out_specs=vmem,
        scratch_shapes=[
            pltpu.VMEM((NROW, units, SRC), bf16),
            pltpu.VMEM((F, SRC), bf16),
            pltpu.VMEM((16, 128), f32),
            pltpu.VMEM((NROW - 1, 16, 128), f32),
            pltpu.VMEM((NZ, 8, 128), f32),
            pltpu.VMEM((NZ - 1, 8, 128), f32),
            pltpu.VMEM((8, 128), f32),
            pltpu.VMEM((NY - 1, 8, 128), f32),
            pltpu.VMEM((TILES * TILE, SRC), bf16),
            pltpu.VMEM((2, 2, 2 * TILE, F), bf16),
            pltpu.VMEM((2, NZ - 1, 2 * TILE, F), bf16),
            pltpu.VMEM((2, 6, 2 * TILE, F), bf16),
            pltpu.VMEM((2, 6, 2 * TILE, F), bf16),
            pltpu.VMEM((NY, TILE, F), bf16),
            pltpu.VMEM((NY - 1, TILE, F), bf16),
            pltpu.VMEM((2, NZ, HALF, F), f32),
            pltpu.VMEM((2, 7, HALF, F), bf16),
            pltpu.VMEM((2, 7, HALF, F), bf16),
            pltpu.VMEM((STEP, F), f32),
            dma((2, 10)),
            dma((2, NROW - 1)),
            dma((2, NZ - 1)),
            dma((2, NY - 1)),
            dma((2, 2, NZ - 1, 2)),
            dma((2, 2, 6)),
            dma((2, NY - 1)),
            dma((2, 2, 7)),
            dma,
        ],
        compiler_params=pltpu.CompilerParams(
            collective_id=0, has_side_effects=True, vmem_limit_bytes=60 * 1024 * 1024
        ),
        name="graph_layer",
    )(features.T, edge_src, edge_dst, tile_count.T, weight, bias[None, :])


def solution(mesh):
    in_specs = (P("col", "row"), P(), P(), P("row", "col"), P("row", "col"), P("row", "col"))
    out_specs = P(("row", "col"), None)
    return jax.shard_map(body, mesh=mesh, in_specs=in_specs, out_specs=out_specs, check_vma=False)
```

```python
import functools

import jax
import jax.numpy as jnp
from jax import lax
from jax.experimental import pallas as pl
from jax.experimental.pallas import tpu as pltpu
from jax.sharding import PartitionSpec as P

TILE = 128
F = 512
SRC = 2048
CAP = 512
TILES = 64
NROW = 8
NY = 4
NZ = 8
HALF = 64
AHEAD = 3
STEP = 1024
bf16 = jnp.bfloat16
f32 = jnp.float32
f8 = jnp.float8_e4m3fn
MESH = pl.DeviceIdType.MESH
NT = (((1,), (1,)), ((), ()))


def onehot(row, size):
    parts = []
    for base in range(0, size, 256):
        width = min(256, size - base)
        value = (row - base).astype(f32).astype(bf16)
        places = lax.broadcasted_iota(jnp.int32, (width, row.shape[1]), 0).astype(f32).astype(bf16)
        parts.append(jnp.where(places == value, jnp.ones((), bf16), jnp.zeros((), bf16)).astype(f8))
    return parts[0] if len(parts) == 1 else jnp.concatenate(parts, axis=0)


def kernel(
    xt, src, dst, cnt, weight, bias, out,
    xg, xs, deg, deg_in, cin, cin_in, cmid, cmid_in, amat,
    zs, zr, ys, yr, p1, p1_in, p2, p2_out, p2_in, acc,
    x_sem, d_sem, c_sem, m_sem, z_sem, y_sem, p1_sem, p2_sem, own_sem,
):
    r = lax.axis_index("row")
    c = lax.axis_index("col")
    y = c // NZ
    z = lax.rem(c, NZ)

    def row_peer(k):
        return (lax.rem(r + k, NROW), c)

    def z_peer(k):
        return (r, y * NZ + lax.rem(z + k, NZ))

    def y_peer(k):
        return (r, lax.rem(y + k, NY) * NZ + z)

    barrier = pltpu.get_barrier_semaphore()
    peers = [row_peer(k) for k in range(1, NROW)]
    peers += [z_peer(k) for k in range(1, NZ)]
    peers += [y_peer(k) for k in range(1, NY)]
    for peer in peers:
        pl.semaphore_signal(barrier, inc=1, device_id=peer, device_id_type=MESH)
    pl.semaphore_wait(barrier, len(peers))

    def remote(source, target, sems, index, peer):
        return pltpu.make_async_remote_copy(
            src_ref=source, dst_ref=target, send_sem=sems.at[(0,) + index],
            recv_sem=sems.at[(1,) + index], device_id=peer, device_id_type=MESH,
        )

    after, before, opposite = (lax.rem(r + k, NROW) for k in (2, 6, 4))
    sibling = (r + 1 - 2 * lax.rem(r, 2), c)
    low, high = pl.ds(0, 32), pl.ds(32, 32)

    def x_copy(index, source, target, peer):
        return remote(source, target, x_sem, (index,), peer)

    right_low = x_copy(0, xt.at[low], xg.at[r, low], (after, c))
    left_high = x_copy(1, xt.at[high], xg.at[r, high], (before, c))
    right_high = x_copy(2, xt.at[high], xg.at[r, high], (after, c))
    left_low = x_copy(3, xt.at[low], xg.at[r, low], (before, c))
    own_across = x_copy(4, xt, xg.at[r], sibling)
    on_right = x_copy(5, xg.at[before, low], xg.at[before, low], (after, c))
    on_left = x_copy(6, xg.at[after, high], xg.at[after, high], (before, c))
    before_across = x_copy(7, xg.at[before], xg.at[before], sibling)
    after_across = x_copy(8, xg.at[after], xg.at[after], sibling)
    opposite_across = x_copy(9, xg.at[opposite], xg.at[opposite], sibling)
    for copy in (right_low, left_high, right_high, left_low, own_across):
        copy.start()
    own = pltpu.make_async_copy(xt, xg.at[r], own_sem)
    own.start()

    slots = lax.broadcasted_iota(jnp.int32, (1, CAP), 1)

    def edges(t):
        return src[pl.ds(t, 1), :], dst[pl.ds(t, 1), :], slots < cnt[0, t]

    def source_step(i, total):
        for j in range(8):
            s, _, valid = edges(i * 8 + j)
            left = onehot(jnp.where(valid, s >> 6, -1), 32)
            total = total + lax.dot_general(left, onehot(s & 63, 64), NT, preferred_element_type=f32)
        return total

    deg[...] = lax.fori_loop(0, TILES // 8, source_step, jnp.zeros((32, 64), f32))
    d_copies = [remote(deg, deg_in.at[k - 1], d_sem, (k - 1,), row_peer(k)) for k in range(1, NROW)]
    for copy in d_copies:
        copy.start()
    right_low.wait_recv()
    on_right.start()
    left_high.wait_recv()
    on_left.start()

    def target_step(zi):
        rows = []
        for j in range(8):
            _, d, valid = edges(2 * ((j // 2) * NZ + zi) + j % 2)
            right = onehot(jnp.where(valid, d, -1), 128)
            rows.append(
                lax.dot_general(jnp.ones((32, CAP), f8), right, NT, preferred_element_type=f32)[:1]
            )
        cin[zi] = jnp.concatenate(rows, axis=0)

    c_copies = [
        remote(cin.at[lax.rem(z + k, NZ)], cin_in.at[k - 1], c_sem, (k - 1,), z_peer(k))
        for k in range(1, NZ)
    ]
    m_copies = [remote(cmid, cmid_in.at[k - 1], m_sem, (k - 1,), y_peer(k)) for k in range(1, NY)]
    def count_matrix(t):
        s, d, valid = edges(t)
        place = jnp.where(valid, (s >> 9) * TILE + d, -1)
        return lax.dot_general(
            onehot(place, 512), onehot(s & 511, 512), NT, preferred_element_type=f32
        ).astype(bf16)

    def build_z(step):
        for jj in range(4):
            zi = lax.rem(z + NZ - 1 - step, NZ) if jj < 2 else lax.rem(z + 1 + step, NZ)
            count = count_matrix(2 * (jj * NZ + zi))
            base = pl.multiple_of(step * STEP + jj * TILE, TILE)
            for h in range(4):
                amat[pl.ds(base, TILE), h * 512 : (h + 1) * 512] = count[h * TILE : (h + 1) * TILE]

    def build_y(group):
        q = group // 2
        d = lax.rem(group, 2)
        yi = lax.rem(y + 2 * NY + (2 * d - 1) * (q + 1), NY)
        for jj in range(4):
            count = count_matrix(2 * (yi * NZ + 4 * d + jj) + 1)
            for part in range(2):
                base = pl.multiple_of((2 * q + part) * STEP + 512 + d * 256 + jj * HALF, HALF)
                for h in range(4):
                    start = h * TILE + part * HALF
                    amat[pl.ds(base, HALF), h * 512 : (h + 1) * 512] = count[start : start + HALF]

    def ahead(step, carry):
        @pl.when(step == 0)
        def _():
            right_high.wait_recv()
            before_across.start()
            left_low.wait_recv()
            after_across.start()

        build_z(step)
        build_y(step + 1)

        @pl.when(step == 0)
        def _():
            on_right.wait_recv()
            on_left.wait_recv()
            opposite_across.start()

        return carry

    build_y(0)
    lax.fori_loop(0, AHEAD, ahead, 0)
    for copy in d_copies:
        copy.wait()
    total = deg[...]
    for k in range(1, NROW):
        total = total + deg_in[k - 1]
    scale = lax.rsqrt(1.0 + total)
    scale = [
        jnp.concatenate([scale[2 * h : 2 * h + 1], scale[2 * h + 1 : 2 * h + 2]], axis=1)
        for h in range(16)
    ]
    own.wait()

    def scale_rows(offset):
        def one(i, carry):
            piece = lax.rem(offset + 2 * i, NROW)
            base = pl.multiple_of(piece * 64, 64)
            for h in range(16):
                cols = slice(h * 128, (h + 1) * 128)
                xs[pl.ds(base, 64), cols] = (xg[piece, :, cols].astype(f32) * scale[h]).astype(bf16)
            return carry

        lax.fori_loop(0, 4, one, 0)

    scale_rows(r)
    for copy in (own_across, before_across, after_across, opposite_across):
        copy.wait_recv()
    scale_rows(r + 1)

    def product(step):
        base = pl.multiple_of(step * STEP, STEP)
        acc[...] = lax.dot_general(
            amat[pl.ds(base, STEP), :], xs[...], NT, preferred_element_type=f32
        )

    def z_copy(d, s, u):
        rows = pl.ds(u * TILE, TILE)
        return remote(
            zs.at[d, lax.rem(s, 2), rows], zr.at[d, s, rows], z_sem, (d, s, u),
            z_peer(1 if d == 0 else NZ - 1),
        )

    def y_copy(d, s):
        return remote(ys.at[d, s], yr.at[d, s], y_sem, (d, s), y_peer(1 if d == 0 else NY - 1))

    def z_sum(d, s, u):
        z_copy(d, s - 1, u).wait_recv()
        rows = slice(d * 256 + u * TILE, d * 256 + (u + 1) * TILE)
        return acc[rows] + zr[d, s - 1, u * TILE : (u + 1) * TILE].astype(f32)

    def z_add(d, s, u):
        acc[d * 256 + u * TILE : d * 256 + (u + 1) * TILE] = z_sum(d, s, u)

    def z_send(d, s, u, value):
        zs[d, lax.rem(s, 2), u * TILE : (u + 1) * TILE] = value.astype(bf16)
        z_copy(d, s, u).start()

    def z_part(d, s, u):
        value = z_sum(d, s, u)

        @pl.when(s > 1)
        def _():
            z_copy(d, s - 2, u).wait_send()

        z_send(d, s, u, value)

    def y_first(d, s):
        ys[d, s] = acc[512 + d * 256 : 768 + d * 256].astype(bf16)
        y_copy(d, s).start()

    def y_part(d, s):
        y_copy(d, s - 2).wait_recv()
        value = acc[512 + d * 256 : 768 + d * 256] + yr[d, s - 2].astype(f32)
        ys[d, s] = value.astype(bf16)
        y_copy(d, s).start()

    def y_last(part):
        for d in range(2):
            y_copy(d, 4 + part).wait_recv()
            for u in range(4):
                first = 512 + d * 256 + u * HALF
                p2[part, 4 * d + u] = acc[first : first + HALF] + yr[
                    d, 4 + part, u * HALF : (u + 1) * HALF
                ].astype(f32)

    def p2_copy(part, slot):
        return remote(
            p2_out.at[part, slot], p2_in.at[part, slot], p2_sem, (part, slot),
            z_peer(1 if slot < 4 else NZ - 1),
        )

    def p2_hop(part, hop):
        for slot in (hop, 4 + hop) if hop < 3 else (hop,):
            zi = lax.rem(z + (4 - hop if slot < 4 else 5 + hop), NZ)
            value = p2[part, zi]
            if hop > 0:
                p2_copy(part, slot - 1).wait_recv()
                value = value + p2_in[part, slot - 1].astype(f32)
            p2_out[part, slot] = value.astype(bf16)
            p2_copy(part, slot).start()

    def ring_step(s, carry):
        @pl.when(s + AHEAD < NZ + 1)
        def _():
            build_z(s + AHEAD - 1)

        @pl.when(s + AHEAD < NZ)
        def _():
            build_y(s + AHEAD)

        product(s)
        for d in range(2):
            z_part(d, s, 0)

        @pl.when(s == 1)
        def _():
            for d in range(2):
                y_first(d, s)

        @pl.when(jnp.logical_and(s > 1, s < 6))
        def _():
            for d in range(2):
                y_part(d, s)

        for d in range(2):
            z_part(d, s, 1)

        @pl.when(s > 4)
        def _():
            def one(i, carry):
                target_step(i)
                return carry

            lax.fori_loop(4 * s - 20, 4 * s - 16, one, 0)

        return carry

    product(0)
    for u in range(2):
        for d in range(2):
            z_send(d, 0, u, acc[d * 256 + u * TILE : d * 256 + (u + 1) * TILE])
            if u == 0:
                y_first(d, 0)
    lax.fori_loop(1, NZ - 1, ring_step, 0)
    for copy in c_copies:
        copy.start()
    y_last(0)
    p2_hop(0, 0)
    product(NZ - 1)
    p2_hop(0, 1)
    y_last(1)
    p2_hop(1, 0)
    for copy in c_copies:
        copy.wait()
    mid = cin[z]
    for k in range(1, NZ):
        mid = mid + cin_in[k - 1]
    cmid[...] = mid
    for copy in m_copies:
        copy.start()
    for d in range(2):
        z_add(d, NZ - 1, 0)
    p2_hop(0, 2)
    p2_hop(1, 1)
    for d in range(2):
        z_add(d, NZ - 1, 1)

    def p1_copy(d, piece):
        return remote(
            p1.at[d, piece], p1_in.at[d, piece], p1_sem, (d, piece), y_peer(1 if d == 0 else NY - 1)
        )

    def p1_send(d, piece):
        yi = lax.rem(y + (2 if piece == 0 else 1 if d == 0 else 3), NY)
        half = d if piece in (0, 2) else 1 - d
        value = acc[pl.ds(pl.multiple_of(yi * TILE + half * HALF, HALF), HALF), :]
        if piece == 2:
            p1_copy(d, 0).wait_recv()
            value = value + p1_in[d, 0].astype(f32)
        p1[d, piece] = value.astype(bf16)
        p1_copy(d, piece).start()

    for piece in range(2):
        for d in range(2):
            p1_send(d, piece)
    p2_hop(0, 3)
    p2_hop(1, 2)
    for d in range(2):
        p1_send(d, 2)
    p2_hop(1, 3)

    for copy in m_copies:
        copy.wait()
    degree = cmid[pl.ds(2 * y, 2), :]
    for k in range(1, NY):
        degree = degree + cmid_in[k - 1, pl.ds(2 * y, 2), :]
    norm = jnp.transpose(lax.rsqrt(1.0 + jnp.concatenate([degree] * 4, axis=0)))

    def finish(half, total):
        normed = (total * norm[:, half : half + 1]).astype(bf16)
        result = jnp.dot(normed, weight[...], preferred_element_type=f32) + bias[...]
        out[half * TILE : (half + 1) * TILE, :] = jnp.maximum(result, 0.0).astype(bf16)

    total = acc[pl.ds(pl.multiple_of(y * TILE, TILE), TILE), :]
    for d in range(2):
        for piece in (1, 2):
            p1_copy(d, piece).wait_recv()
        order = (2, 1) if d == 0 else (1, 2)
        total = total + jnp.concatenate([p1_in[d, piece] for piece in order], axis=0).astype(f32)
    finish(0, total)
    totals = []
    for part in range(2):
        total = p2[part, z]
        for slot in (3, 6):
            p2_copy(part, slot).wait_recv()
            total = total + p2_in[part, slot].astype(f32)
        totals.append(total)
    finish(1, jnp.concatenate(totals, axis=0))

    for copy in (
        right_low, left_high, right_high, left_low, own_across,
        on_right, on_left, before_across, after_across, opposite_across,
    ):
        copy.wait_send()
    for d in range(2):
        for s in (NZ - 3, NZ - 2):
            for u in range(2):
                z_copy(d, s, u).wait_send()
        for s in range(6):
            y_copy(d, s).wait_send()
    for part in range(2):
        for slot in range(7):
            p2_copy(part, slot).wait_send()
    for d in range(2):
        for piece in range(3):
            p1_copy(d, piece).wait_send()


def body(features, weight, bias, edge_src, edge_dst, tile_count):
    vmem = pl.BlockSpec(memory_space=pltpu.VMEM)
    smem = pl.BlockSpec(memory_space=pltpu.SMEM)
    units = features.shape[1]
    dma = pltpu.SemaphoreType.DMA
    return pl.pallas_call(
        kernel,
        out_shape=jax.ShapeDtypeStruct((2 * TILE, F), bf16),
        in_specs=[vmem, vmem, vmem, smem, vmem, vmem],
        out_specs=vmem,
        scratch_shapes=[
            pltpu.VMEM((NROW, units, SRC), bf16),
            pltpu.VMEM((F, SRC), bf16),
            pltpu.VMEM((32, 64), f32),
            pltpu.VMEM((NROW - 1, 32, 64), f32),
            pltpu.VMEM((NZ, 8, 128), f32),
            pltpu.VMEM((NZ - 1, 8, 128), f32),
            pltpu.VMEM((8, 128), f32),
            pltpu.VMEM((NY - 1, 8, 128), f32),
            pltpu.VMEM((TILES * TILE, SRC), bf16),
            pltpu.VMEM((2, 2, 2 * TILE, F), bf16),
            pltpu.VMEM((2, NZ - 1, 2 * TILE, F), bf16),
            pltpu.VMEM((2, 6, 2 * TILE, F), bf16),
            pltpu.VMEM((2, 6, 2 * TILE, F), bf16),
            pltpu.VMEM((2, 3, HALF, F), bf16),
            pltpu.VMEM((2, 3, HALF, F), bf16),
            pltpu.VMEM((2, NZ, HALF, F), f32),
            pltpu.VMEM((2, 7, HALF, F), bf16),
            pltpu.VMEM((2, 7, HALF, F), bf16),
            pltpu.VMEM((STEP, F), f32),
            dma((2, 10)),
            dma((2, NROW - 1)),
            dma((2, NZ - 1)),
            dma((2, NY - 1)),
            dma((2, 2, NZ - 1, 2)),
            dma((2, 2, 6)),
            dma((2, 2, 3)),
            dma((2, 2, 7)),
            dma,
        ],
        compiler_params=pltpu.CompilerParams(
            collective_id=0, has_side_effects=True, vmem_limit_bytes=60 * 1024 * 1024
        ),
        name="graph_layer",
    )(features.T, edge_src, edge_dst, tile_count.T, weight, bias[None, :])


def solution(mesh):
    in_specs = (P("col", "row"), P(), P(), P("row", "col"), P("row", "col"), P("row", "col"))
    out_specs = P(("row", "col"), None)
    return jax.shard_map(body, mesh=mesh, in_specs=in_specs, out_specs=out_specs, check_vma=False)
```

```python
import functools

import jax
import jax.numpy as jnp
from jax import lax
from jax.experimental import pallas as pl
from jax.experimental.pallas import tpu as pltpu
from jax.sharding import PartitionSpec as P

TILE = 128
F = 512
SRC = 2048
CAP = 512
TILES = 64
NROW = 8
NY = 4
NZ = 8
HALF = 64
AHEAD = 3
STEP = 1024
bf16 = jnp.bfloat16
f32 = jnp.float32
f8 = jnp.float8_e4m3fn
MESH = pl.DeviceIdType.MESH
NT = (((1,), (1,)), ((), ()))


def onehot(row, size):
    parts = []
    for base in range(0, size, 256):
        width = min(256, size - base)
        value = (row - base).astype(f32).astype(bf16)
        places = lax.broadcasted_iota(jnp.int32, (width, row.shape[1]), 0).astype(f32).astype(bf16)
        parts.append(jnp.where(places == value, jnp.ones((), bf16), jnp.zeros((), bf16)).astype(f8))
    return parts[0] if len(parts) == 1 else jnp.concatenate(parts, axis=0)


def kernel(
    xt, src, dst, cnt, weight, bias, out,
    xg, xs, deg, deg_in, cin, cin_in, cmid, cmid_in, amat,
    zs, zr, ys, yr, p1, p1_in, p2, p2_out, p2_in, acc, acc_y,
    x_sem, d_sem, c_sem, m_sem, z_sem, y_sem, p1_sem, p2_sem, own_sem,
):
    r = lax.axis_index("row")
    c = lax.axis_index("col")
    y = c // NZ
    z = lax.rem(c, NZ)

    def row_peer(k):
        return (lax.rem(r + k, NROW), c)

    def z_peer(k):
        return (r, y * NZ + lax.rem(z + k, NZ))

    def y_peer(k):
        return (r, lax.rem(y + k, NY) * NZ + z)

    barrier = pltpu.get_barrier_semaphore()
    peers = [row_peer(k) for k in range(1, NROW)]
    peers += [z_peer(k) for k in range(1, NZ)]
    peers += [y_peer(k) for k in range(1, NY)]
    for peer in peers:
        pl.semaphore_signal(barrier, inc=1, device_id=peer, device_id_type=MESH)
    pl.semaphore_wait(barrier, len(peers))

    def remote(source, target, sems, index, peer):
        return pltpu.make_async_remote_copy(
            src_ref=source, dst_ref=target, send_sem=sems.at[(0,) + index],
            recv_sem=sems.at[(1,) + index], device_id=peer, device_id_type=MESH,
        )

    after, before, opposite = (lax.rem(r + k, NROW) for k in (2, 6, 4))
    sibling = (r + 1 - 2 * lax.rem(r, 2), c)
    low, high = pl.ds(0, 32), pl.ds(32, 32)

    def x_copy(index, source, target, peer):
        return remote(source, target, x_sem, (index,), peer)

    right_low = x_copy(0, xt.at[low], xg.at[r, low], (after, c))
    left_high = x_copy(1, xt.at[high], xg.at[r, high], (before, c))
    right_high = x_copy(2, xt.at[high], xg.at[r, high], (after, c))
    left_low = x_copy(3, xt.at[low], xg.at[r, low], (before, c))
    own_across = x_copy(4, xt, xg.at[r], sibling)
    on_right = x_copy(5, xg.at[before, low], xg.at[before, low], (after, c))
    on_left = x_copy(6, xg.at[after, high], xg.at[after, high], (before, c))
    before_across = x_copy(7, xg.at[before], xg.at[before], sibling)
    after_across = x_copy(8, xg.at[after], xg.at[after], sibling)
    opposite_across = x_copy(9, xg.at[opposite], xg.at[opposite], sibling)
    for copy in (right_low, left_high, own_across):
        copy.start()
    own = pltpu.make_async_copy(xt, xg.at[r], own_sem)
    own.start()

    slots = lax.broadcasted_iota(jnp.int32, (1, CAP), 1)

    def edges(t):
        return src[pl.ds(t, 1), :], dst[pl.ds(t, 1), :], slots < cnt[0, t]

    def source_step(i, total):
        for j in range(8):
            s, _, valid = edges(i * 8 + j)
            left = onehot(jnp.where(valid, s >> 6, -1), 32)
            total = total + lax.dot_general(left, onehot(s & 63, 64), NT, preferred_element_type=f32)
        return total

    deg[...] = lax.fori_loop(0, TILES // 8, source_step, jnp.zeros((32, 64), f32))
    d_copies = [remote(deg, deg_in.at[k - 1], d_sem, (k - 1,), row_peer(k)) for k in range(1, NROW)]
    for copy in d_copies:
        copy.start()
    right_low.wait_recv()
    on_right.start()
    left_high.wait_recv()
    on_left.start()
    right_high.start()
    left_low.start()

    def target_step(zi):
        rows = []
        for j in range(8):
            _, d, valid = edges(2 * ((j // 2) * NZ + zi) + j % 2)
            right = onehot(jnp.where(valid, d, -1), 128)
            rows.append(
                lax.dot_general(jnp.ones((32, CAP), f8), right, NT, preferred_element_type=f32)[:1]
            )
        cin[zi] = jnp.concatenate(rows, axis=0)

    def target_steps(first):
        def one(i, carry):
            target_step(i)
            return carry

        lax.fori_loop(first, first + 4, one, 0)

    c_copies = [
        remote(cin.at[lax.rem(z + k, NZ)], cin_in.at[k - 1], c_sem, (k - 1,), z_peer(k))
        for k in range(1, NZ)
    ]
    m_copies = [remote(cmid, cmid_in.at[k - 1], m_sem, (k - 1,), y_peer(k)) for k in range(1, NY)]
    def count_matrix(t):
        s, d, valid = edges(t)
        place = jnp.where(valid, (s >> 9) * TILE + d, -1)
        return lax.dot_general(
            onehot(place, 512), onehot(s & 511, 512), NT, preferred_element_type=f32
        ).astype(bf16)

    def build_z(step):
        for jj in range(4):
            zi = lax.rem(z + NZ - 1 - step, NZ) if jj < 2 else lax.rem(z + 1 + step, NZ)
            count = count_matrix(2 * (jj * NZ + zi))
            base = pl.multiple_of(step * STEP + jj * TILE, TILE)
            for h in range(4):
                amat[pl.ds(base, TILE), h * 512 : (h + 1) * 512] = count[h * TILE : (h + 1) * TILE]

    def build_y(group):
        q = group // 2
        d = lax.rem(group, 2)
        yi = lax.rem(y + 2 * NY + (2 * d - 1) * (q + 1), NY)
        for jj in range(4):
            count = count_matrix(2 * (yi * NZ + 4 * d + jj) + 1)
            for part in range(2):
                base = pl.multiple_of((2 * q + part) * STEP + 512 + d * 256 + jj * HALF, HALF)
                for h in range(4):
                    start = h * TILE + part * HALF
                    amat[pl.ds(base, HALF), h * 512 : (h + 1) * 512] = count[start : start + HALF]

    def ahead(step, carry):
        @pl.when(step == 0)
        def _():
            right_high.wait_recv()
            before_across.start()
            left_low.wait_recv()
            after_across.start()

        build_z(step)
        build_y(step + 1)

        @pl.when(step == 0)
        def _():
            on_right.wait_recv()
            on_left.wait_recv()
            opposite_across.start()

        return carry

    build_y(0)
    lax.fori_loop(0, AHEAD, ahead, 0)
    target_steps(0)
    for copy in d_copies:
        copy.wait()
    total = deg[...]
    for k in range(1, NROW):
        total = total + deg_in[k - 1]
    scale = lax.rsqrt(1.0 + total)
    scale = [
        jnp.concatenate([scale[2 * h : 2 * h + 1], scale[2 * h + 1 : 2 * h + 2]], axis=1)
        for h in range(16)
    ]
    own.wait()

    def scale_rows(offset):
        def one(i, carry):
            piece = lax.rem(offset + 2 * i, NROW)
            base = pl.multiple_of(piece * 64, 64)
            for h in range(16):
                cols = slice(h * 128, (h + 1) * 128)
                xs[pl.ds(base, 64), cols] = (xg[piece, :, cols].astype(f32) * scale[h]).astype(bf16)
            return carry

        lax.fori_loop(0, 4, one, 0)

    scale_rows(r)
    for copy in (own_across, before_across, after_across, opposite_across):
        copy.wait_recv()
    scale_rows(r + 1)

    def product(first, rows, target):
        base = pl.multiple_of(first, 512)
        target[:rows, :] = lax.dot_general(
            amat[pl.ds(base, rows), :], xs[...], NT, preferred_element_type=f32
        )

    def z_copy(d, s, u):
        rows = pl.ds(u * TILE, TILE)
        return remote(
            zs.at[d, lax.rem(s, 2), rows], zr.at[d, s, rows], z_sem, (d, s, u),
            z_peer(1 if d == 0 else NZ - 1),
        )

    def y_copy(d, s):
        return remote(ys.at[d, s], yr.at[d, s], y_sem, (d, s), y_peer(1 if d == 0 else NY - 1))

    def z_sum(d, s, u):
        z_copy(d, s - 1, u).wait_recv()
        rows = slice(d * 256 + u * TILE, d * 256 + (u + 1) * TILE)
        return acc[rows] + zr[d, s - 1, u * TILE : (u + 1) * TILE].astype(f32)

    def z_add(d, s, u):
        acc[d * 256 + u * TILE : d * 256 + (u + 1) * TILE] = z_sum(d, s, u)

    def z_send(d, s, u, value):
        zs[d, lax.rem(s, 2), u * TILE : (u + 1) * TILE] = value.astype(bf16)
        z_copy(d, s, u).start()

    def z_part(d, s, u):
        value = z_sum(d, s, u)

        if isinstance(s, int):
            z_copy(d, s - 2, u).wait_send()
        else:

            @pl.when(s > 1)
            def _():
                z_copy(d, s - 2, u).wait_send()

        z_send(d, s, u, value)

    def y_first(d, s):
        ys[d, s] = acc[512 + d * 256 : 768 + d * 256].astype(bf16)
        y_copy(d, s).start()

    def y_part(d, s):
        y_copy(d, s - 2).wait_recv()
        value = acc[512 + d * 256 : 768 + d * 256] + yr[d, s - 2].astype(f32)
        ys[d, s] = value.astype(bf16)
        y_copy(d, s).start()

    def y_last(part, source, offset):
        for d in range(2):
            y_copy(d, 4 + part).wait_recv()
            for u in range(4):
                first = offset + d * 256 + u * HALF
                p2[part, 4 * d + u] = source[first : first + HALF] + yr[
                    d, 4 + part, u * HALF : (u + 1) * HALF
                ].astype(f32)

    def p2_copy(part, slot):
        return remote(
            p2_out.at[part, slot], p2_in.at[part, slot], p2_sem, (part, slot),
            z_peer(1 if slot < 4 else NZ - 1),
        )

    def p2_hop(part, hop):
        for slot in (hop, 4 + hop) if hop < 3 else (hop,):
            zi = lax.rem(z + (4 - hop if slot < 4 else 5 + hop), NZ)
            value = p2[part, zi]
            if hop > 0:
                p2_copy(part, slot - 1).wait_recv()
                value = value + p2_in[part, slot - 1].astype(f32)
            p2_out[part, slot] = value.astype(bf16)
            p2_copy(part, slot).start()

    def ring_step(s, carry):
        @pl.when(s + AHEAD < NZ + 1)
        def _():
            build_z(s + AHEAD - 1)

        @pl.when(s + AHEAD < NZ)
        def _():
            build_y(s + AHEAD)

        product(s * STEP, STEP, acc)
        for d in range(2):
            z_part(d, s, 0)

        @pl.when(s == 1)
        def _():
            for d in range(2):
                y_first(d, s)

        @pl.when(s > 1)
        def _():
            for d in range(2):
                y_part(d, s)

        for d in range(2):
            z_part(d, s, 1)
        return carry

    product(0, STEP, acc)
    for u in range(2):
        for d in range(2):
            z_send(d, 0, u, acc[d * 256 + u * TILE : d * 256 + (u + 1) * TILE])
            if u == 0:
                y_first(d, 0)
    lax.fori_loop(1, NZ - 2, ring_step, 0)
    target_steps(4)
    for copy in c_copies:
        copy.start()
    product((NZ - 2) * STEP, STEP, acc)
    for d in range(2):
        z_part(d, NZ - 2, 0)
    y_last(0, acc, 512)
    p2_hop(0, 0)
    for d in range(2):
        z_part(d, NZ - 2, 1)
    product((NZ - 1) * STEP + 512, 512, acc_y)
    p2_hop(0, 1)
    y_last(1, acc_y, 0)
    p2_hop(1, 0)
    product((NZ - 1) * STEP, 512, acc)
    for copy in c_copies:
        copy.wait()
    mid = cin[z]
    for k in range(1, NZ):
        mid = mid + cin_in[k - 1]
    cmid[...] = mid
    for copy in m_copies:
        copy.start()
    for d in range(2):
        z_add(d, NZ - 1, 0)
    p2_hop(0, 2)
    p2_hop(1, 1)
    for d in range(2):
        z_add(d, NZ - 1, 1)

    def p1_copy(d, piece):
        return remote(
            p1.at[d, piece], p1_in.at[d, piece], p1_sem, (d, piece), y_peer(1 if d == 0 else NY - 1)
        )

    def p1_send(d, piece):
        yi = lax.rem(y + (2 if piece == 0 else 1 if d == 0 else 3), NY)
        half = d if piece in (0, 2) else 1 - d
        value = acc[pl.ds(pl.multiple_of(yi * TILE + half * HALF, HALF), HALF), :]
        if piece == 2:
            p1_copy(d, 0).wait_recv()
            value = value + p1_in[d, 0].astype(f32)
        p1[d, piece] = value.astype(bf16)
        p1_copy(d, piece).start()

    for piece in range(2):
        for d in range(2):
            p1_send(d, piece)
    p2_hop(0, 3)
    p2_hop(1, 2)
    for d in range(2):
        p1_send(d, 2)
    p2_hop(1, 3)

    for copy in m_copies:
        copy.wait()
    degree = cmid[pl.ds(2 * y, 2), :]
    for k in range(1, NY):
        degree = degree + cmid_in[k - 1, pl.ds(2 * y, 2), :]
    norm = jnp.transpose(lax.rsqrt(1.0 + jnp.concatenate([degree] * 4, axis=0)))

    def finish(half, total):
        normed = (total * norm[:, half : half + 1]).astype(bf16)
        result = jnp.dot(normed, weight[...], preferred_element_type=f32) + bias[...]
        out[half * TILE : (half + 1) * TILE, :] = jnp.maximum(result, 0.0).astype(bf16)

    total = acc[pl.ds(pl.multiple_of(y * TILE, TILE), TILE), :]
    for d in range(2):
        for piece in (1, 2):
            p1_copy(d, piece).wait_recv()
        order = (2, 1) if d == 0 else (1, 2)
        total = total + jnp.concatenate([p1_in[d, piece] for piece in order], axis=0).astype(f32)
    finish(0, total)
    totals = []
    for part in range(2):
        total = p2[part, z]
        for slot in (3, 6):
            p2_copy(part, slot).wait_recv()
            total = total + p2_in[part, slot].astype(f32)
        totals.append(total)
    finish(1, jnp.concatenate(totals, axis=0))

    for copy in (
        right_low, left_high, right_high, left_low, own_across,
        on_right, on_left, before_across, after_across, opposite_across,
    ):
        copy.wait_send()
    for d in range(2):
        for s in (NZ - 3, NZ - 2):
            for u in range(2):
                z_copy(d, s, u).wait_send()
        for s in range(6):
            y_copy(d, s).wait_send()
    for part in range(2):
        for slot in range(7):
            p2_copy(part, slot).wait_send()
    for d in range(2):
        for piece in range(3):
            p1_copy(d, piece).wait_send()


def body(features, weight, bias, edge_src, edge_dst, tile_count):
    vmem = pl.BlockSpec(memory_space=pltpu.VMEM)
    smem = pl.BlockSpec(memory_space=pltpu.SMEM)
    units = features.shape[1]
    dma = pltpu.SemaphoreType.DMA
    return pl.pallas_call(
        kernel,
        out_shape=jax.ShapeDtypeStruct((2 * TILE, F), bf16),
        in_specs=[vmem, vmem, vmem, smem, vmem, vmem],
        out_specs=vmem,
        scratch_shapes=[
            pltpu.VMEM((NROW, units, SRC), bf16),
            pltpu.VMEM((F, SRC), bf16),
            pltpu.VMEM((32, 64), f32),
            pltpu.VMEM((NROW - 1, 32, 64), f32),
            pltpu.VMEM((NZ, 8, 128), f32),
            pltpu.VMEM((NZ - 1, 8, 128), f32),
            pltpu.VMEM((8, 128), f32),
            pltpu.VMEM((NY - 1, 8, 128), f32),
            pltpu.VMEM((TILES * TILE, SRC), bf16),
            pltpu.VMEM((2, 2, 2 * TILE, F), bf16),
            pltpu.VMEM((2, NZ - 1, 2 * TILE, F), bf16),
            pltpu.VMEM((2, 6, 2 * TILE, F), bf16),
            pltpu.VMEM((2, 6, 2 * TILE, F), bf16),
            pltpu.VMEM((2, 3, HALF, F), bf16),
            pltpu.VMEM((2, 3, HALF, F), bf16),
            pltpu.VMEM((2, NZ, HALF, F), f32),
            pltpu.VMEM((2, 7, HALF, F), bf16),
            pltpu.VMEM((2, 7, HALF, F), bf16),
            pltpu.VMEM((STEP, F), f32),
            pltpu.VMEM((STEP // 2, F), f32),
            dma((2, 10)),
            dma((2, NROW - 1)),
            dma((2, NZ - 1)),
            dma((2, NY - 1)),
            dma((2, 2, NZ - 1, 2)),
            dma((2, 2, 6)),
            dma((2, 2, 3)),
            dma((2, 2, 7)),
            dma,
        ],
        compiler_params=pltpu.CompilerParams(
            collective_id=0, has_side_effects=True, vmem_limit_bytes=60 * 1024 * 1024
        ),
        name="graph_layer",
    )(features.T, edge_src, edge_dst, tile_count.T, weight, bias[None, :])


def solution(mesh):
    in_specs = (P("col", "row"), P(), P(), P("row", "col"), P("row", "col"), P("row", "col"))
    out_specs = P(("row", "col"), None)
    return jax.shard_map(body, mesh=mesh, in_specs=in_specs, out_specs=out_specs, check_vma=False)
```

```python
import functools

import jax
import jax.numpy as jnp
from jax import lax
from jax.experimental import pallas as pl
from jax.experimental.pallas import tpu as pltpu
from jax.sharding import PartitionSpec as P

TILE = 128
F = 512
SRC = 2048
CAP = 512
TILES = 64
NROW = 8
NY = 4
NZ = 8
HALF = 64
AHEAD = 2
STEP = 1024
bf16 = jnp.bfloat16
f32 = jnp.float32
f8 = jnp.float8_e4m3fn
MESH = pl.DeviceIdType.MESH
NT = (((1,), (1,)), ((), ()))


def onehot(row, size):
    parts = []
    for base in range(0, size, 256):
        width = min(256, size - base)
        value = (row - base).astype(f32).astype(bf16)
        places = lax.broadcasted_iota(jnp.int32, (width, row.shape[1]), 0).astype(f32).astype(bf16)
        parts.append(jnp.where(places == value, jnp.ones((), bf16), jnp.zeros((), bf16)).astype(f8))
    return parts[0] if len(parts) == 1 else jnp.concatenate(parts, axis=0)


def kernel(
    xt, src, dst, cnt, weight, bias, out,
    xg, xs, deg, deg_in, cin, cin_in, cmid, cmid_in, amat,
    zs, zr, ys, yr, p1, p1_in, p2, p2_out, p2_in, acc, acc_y,
    x_sem, d_sem, c_sem, m_sem, z_sem, y_sem, p1_sem, p2_sem, own_sem,
):
    r = lax.axis_index("row")
    c = lax.axis_index("col")
    y = c // NZ
    z = lax.rem(c, NZ)

    def row_peer(k):
        return (lax.rem(r + k, NROW), c)

    def z_peer(k):
        return (r, y * NZ + lax.rem(z + k, NZ))

    def y_peer(k):
        return (r, lax.rem(y + k, NY) * NZ + z)

    barrier = pltpu.get_barrier_semaphore()
    peers = [row_peer(k) for k in range(1, NROW)]
    peers += [z_peer(k) for k in range(1, NZ)]
    peers += [y_peer(k) for k in range(1, NY)]
    for peer in peers:
        pl.semaphore_signal(barrier, inc=1, device_id=peer, device_id_type=MESH)
    pl.semaphore_wait(barrier, len(peers))

    def remote(source, target, sems, index, peer):
        return pltpu.make_async_remote_copy(
            src_ref=source, dst_ref=target, send_sem=sems.at[(0,) + index],
            recv_sem=sems.at[(1,) + index], device_id=peer, device_id_type=MESH,
        )

    after, before, opposite = (lax.rem(r + k, NROW) for k in (2, 6, 4))
    sibling = (r + 1 - 2 * lax.rem(r, 2), c)
    low, high = pl.ds(0, 32), pl.ds(32, 32)

    def x_copy(index, source, target, peer):
        return remote(source, target, x_sem, (index,), peer)

    right_low = x_copy(0, xt.at[low], xg.at[r, low], (after, c))
    left_high = x_copy(1, xt.at[high], xg.at[r, high], (before, c))
    right_high = x_copy(2, xt.at[high], xg.at[r, high], (after, c))
    left_low = x_copy(3, xt.at[low], xg.at[r, low], (before, c))
    own_across = x_copy(4, xt, xg.at[r], sibling)
    on_right = x_copy(5, xg.at[before, low], xg.at[before, low], (after, c))
    on_left = x_copy(6, xg.at[after, high], xg.at[after, high], (before, c))
    before_across = x_copy(7, xg.at[before], xg.at[before], sibling)
    after_across = x_copy(8, xg.at[after], xg.at[after], sibling)
    opposite_across = x_copy(9, xg.at[opposite], xg.at[opposite], sibling)
    for copy in (right_low, left_high, own_across):
        copy.start()
    own = pltpu.make_async_copy(xt, xg.at[r], own_sem)
    own.start()

    slots = lax.broadcasted_iota(jnp.int32, (1, CAP), 1)

    def edges(t):
        return src[pl.ds(t, 1), :], dst[pl.ds(t, 1), :], slots < cnt[0, t]

    def source_step(i, total):
        for j in range(8):
            s, _, valid = edges(i * 8 + j)
            left = onehot(jnp.where(valid, s >> 6, -1), 32)
            total = total + lax.dot_general(left, onehot(s & 63, 64), NT, preferred_element_type=f32)
        return total

    deg[...] = lax.fori_loop(0, TILES // 8, source_step, jnp.zeros((32, 64), f32))
    d_copies = [remote(deg, deg_in.at[k - 1], d_sem, (k - 1,), row_peer(k)) for k in range(1, NROW)]
    for copy in d_copies:
        copy.start()
    right_low.wait_recv()
    on_right.start()
    left_high.wait_recv()
    on_left.start()
    right_high.start()
    left_low.start()

    def target_step(zi):
        rows = []
        for j in range(8):
            _, d, valid = edges(2 * ((j // 2) * NZ + zi) + j % 2)
            right = onehot(jnp.where(valid, d, -1), 128)
            rows.append(
                lax.dot_general(jnp.ones((32, CAP), f8), right, NT, preferred_element_type=f32)[:1]
            )
        cin[zi] = jnp.concatenate(rows, axis=0)

    def target_steps(first):
        def one(i, carry):
            target_step(i)
            return carry

        lax.fori_loop(first, first + 4, one, 0)

    c_copies = [
        remote(cin.at[lax.rem(z + k, NZ)], cin_in.at[k - 1], c_sem, (k - 1,), z_peer(k))
        for k in range(1, NZ)
    ]
    m_copies = [remote(cmid, cmid_in.at[k - 1], m_sem, (k - 1,), y_peer(k)) for k in range(1, NY)]
    def count_matrix(t):
        s, d, valid = edges(t)
        place = jnp.where(valid, (s >> 9) * TILE + d, -1)
        return lax.dot_general(
            onehot(place, 512), onehot(s & 511, 512), NT, preferred_element_type=f32
        ).astype(bf16)

    def build(p):
        group = p // 2
        is_y = lax.rem(p, 2)
        q = group // 2
        d = lax.rem(group, 2)
        yi = lax.rem(y + 2 * NY + (2 * d - 1) * (q + 1), NY)
        for jj in range(4):
            zi = lax.rem(z + NZ - 1 - group, NZ) if jj < 2 else lax.rem(z + 1 + group, NZ)
            z_tile = 2 * (jj * NZ + zi)
            y_tile = 2 * (yi * NZ + 4 * d + jj) + 1
            count = count_matrix(z_tile + is_y * (y_tile - z_tile))
            z_base = group * STEP + jj * TILE
            y_base = 2 * q * STEP + 512 + d * 256 + jj * HALF
            base = z_base + is_y * (y_base - z_base)
            for part in range(2):
                first = pl.multiple_of(base + part * (HALF + is_y * (STEP - HALF)), HALF)
                for h in range(4):
                    start = h * TILE + part * HALF
                    amat[pl.ds(first, HALF), h * 512 : (h + 1) * 512] = count[start : start + HALF]

    def ahead(p, carry):
        @pl.when(p == 2)
        def _():
            right_high.wait_recv()
            before_across.start()
            left_low.wait_recv()
            after_across.start()

        @pl.when(p == 3)
        def _():
            on_right.wait_recv()
            on_left.wait_recv()
            opposite_across.start()

        build(p)
        return carry

    lax.fori_loop(0, 2 * AHEAD + 2, ahead, 0)
    target_steps(0)
    for copy in d_copies:
        copy.wait()
    total = deg[...]
    for k in range(1, NROW):
        total = total + deg_in[k - 1]
    scale = lax.rsqrt(1.0 + total)
    scale = [
        jnp.concatenate([scale[2 * h : 2 * h + 1], scale[2 * h + 1 : 2 * h + 2]], axis=1)
        for h in range(16)
    ]
    own.wait()

    def scale_rows(offset):
        def one(i, carry):
            piece = lax.rem(offset + 2 * i, NROW)
            base = pl.multiple_of(piece * 64, 64)
            for h in range(16):
                cols = slice(h * 128, (h + 1) * 128)
                xs[pl.ds(base, 64), cols] = (xg[piece, :, cols].astype(f32) * scale[h]).astype(bf16)
            return carry

        lax.fori_loop(0, 4, one, 0)

    scale_rows(r)
    for copy in (own_across, before_across, after_across, opposite_across):
        copy.wait_recv()
    scale_rows(r + 1)

    def product(first, rows, target):
        def one(i, carry):
            base = pl.multiple_of(first + i * 512, 512)
            target[pl.ds(pl.multiple_of(i * 512, 512), 512), :] = lax.dot_general(
                amat[pl.ds(base, 512), :], xs[...], NT, preferred_element_type=f32
            )
            return carry

        lax.fori_loop(0, rows // 512, one, 0)

    def z_copy(d, s, u):
        rows = pl.ds(u * TILE, TILE)
        return remote(
            zs.at[d, lax.rem(s, 2), rows], zr.at[d, s, rows], z_sem, (d, s, u),
            z_peer(1 if d == 0 else NZ - 1),
        )

    def y_copy(d, s):
        return remote(ys.at[d, s], yr.at[d, s], y_sem, (d, s), y_peer(1 if d == 0 else NY - 1))

    def z_sum(d, s, u):
        z_copy(d, s - 1, u).wait_recv()
        rows = slice(d * 256 + u * TILE, d * 256 + (u + 1) * TILE)
        return acc[rows] + zr[d, s - 1, u * TILE : (u + 1) * TILE].astype(f32)

    def z_add(d, s, u):
        acc[d * 256 + u * TILE : d * 256 + (u + 1) * TILE] = z_sum(d, s, u)

    def z_send(d, s, u, value):
        zs[d, lax.rem(s, 2), u * TILE : (u + 1) * TILE] = value.astype(bf16)
        z_copy(d, s, u).start()

    def z_part(d, s, u):
        value = z_sum(d, s, u)

        @pl.when(s > 1)
        def _():
            z_copy(d, s - 2, u).wait_send()

        z_send(d, s, u, value)

    def y_first(d, s):
        ys[d, s] = acc[512 + d * 256 : 768 + d * 256].astype(bf16)
        y_copy(d, s).start()

    def y_part(d, s):
        y_copy(d, s - 2).wait_recv()
        value = acc[512 + d * 256 : 768 + d * 256] + yr[d, s - 2].astype(f32)
        ys[d, s] = value.astype(bf16)
        y_copy(d, s).start()

    def y_last(part, source, offset):
        for d in range(2):
            y_copy(d, 4 + part).wait_recv()
            for u in range(4):
                first = offset + d * 256 + u * HALF
                p2[part, 4 * d + u] = source[first : first + HALF] + yr[
                    d, 4 + part, u * HALF : (u + 1) * HALF
                ].astype(f32)

    def p2_copy(part, slot):
        return remote(
            p2_out.at[part, slot], p2_in.at[part, slot], p2_sem, (part, slot),
            z_peer(1 if slot < 4 else NZ - 1),
        )

    def p2_hop(part, hop):
        for slot in (hop, 4 + hop) if hop < 3 else (hop,):
            zi = lax.rem(z + (4 - hop if slot < 4 else 5 + hop), NZ)
            value = p2[part, zi]
            if hop > 0:
                p2_copy(part, slot - 1).wait_recv()
                value = value + p2_in[part, slot - 1].astype(f32)
            p2_out[part, slot] = value.astype(bf16)
            p2_copy(part, slot).start()

    def ring_step(s, carry):
        sends = s > 0

        @pl.when(jnp.logical_and(s > 0, s < NZ - AHEAD))
        def _():
            def one(p, carry):
                build(p)
                return carry

            lax.fori_loop(2 * (s + AHEAD), 2 * (s + AHEAD) + 2, one, 0)

        @pl.when(s == NZ - 2)
        def _():
            target_steps(4)
            for copy in c_copies:
                copy.start()

        product(s * STEP, STEP, acc)

        @pl.when(s == 0)
        def _():
            for u in range(2):
                for d in range(2):
                    z_send(d, s, u, acc[d * 256 + u * TILE : d * 256 + (u + 1) * TILE])

        @pl.when(sends)
        def _():
            for d in range(2):
                z_part(d, s, 0)

        @pl.when(s < 2)
        def _():
            for d in range(2):
                y_first(d, s)

        @pl.when(jnp.logical_and(s > 1, s < 6))
        def _():
            for d in range(2):
                y_part(d, s)

        @pl.when(s == 6)
        def _():
            y_last(0, acc, 512)
            p2_hop(0, 0)
            product((NZ - 1) * STEP + 512, 512, acc_y)

        @pl.when(sends)
        def _():
            for d in range(2):
                z_part(d, s, 1)

        return carry

    lax.fori_loop(0, NZ - 1, ring_step, 0)
    y_last(1, acc_y, 0)
    p2_hop(1, 0)
    p2_hop(0, 1)
    product((NZ - 1) * STEP, 512, acc)
    for copy in c_copies:
        copy.wait()
    mid = cin[z]
    for k in range(1, NZ):
        mid = mid + cin_in[k - 1]
    cmid[...] = mid
    for copy in m_copies:
        copy.start()
    for d in range(2):
        z_add(d, NZ - 1, 0)
    p2_hop(0, 2)
    p2_hop(1, 1)
    for d in range(2):
        z_add(d, NZ - 1, 1)

    def p1_copy(d, piece):
        return remote(
            p1.at[d, piece], p1_in.at[d, piece], p1_sem, (d, piece), y_peer(1 if d == 0 else NY - 1)
        )

    def p1_send(d, piece):
        yi = lax.rem(y + (2 if piece == 0 else 1 if d == 0 else 3), NY)
        half = d if piece in (0, 2) else 1 - d
        value = acc[pl.ds(pl.multiple_of(yi * TILE + half * HALF, HALF), HALF), :]
        if piece == 2:
            p1_copy(d, 0).wait_recv()
            value = value + p1_in[d, 0].astype(f32)
        p1[d, piece] = value.astype(bf16)
        p1_copy(d, piece).start()

    for piece in range(2):
        for d in range(2):
            p1_send(d, piece)
    p2_hop(0, 3)
    p2_hop(1, 2)
    for d in range(2):
        p1_send(d, 2)
    p2_hop(1, 3)

    for copy in m_copies:
        copy.wait()
    degree = cmid[pl.ds(2 * y, 2), :]
    for k in range(1, NY):
        degree = degree + cmid_in[k - 1, pl.ds(2 * y, 2), :]
    norm = jnp.transpose(lax.rsqrt(1.0 + jnp.concatenate([degree] * 4, axis=0)))

    def finish(first, total):
        rows = total.shape[0]
        half, start = first // TILE, first % TILE
        normed = (total * norm[start : start + rows, half : half + 1]).astype(bf16)
        result = jnp.dot(normed, weight[...], preferred_element_type=f32) + bias[...]
        out[first : first + rows, :] = jnp.maximum(result, 0.0).astype(bf16)

    total = acc[pl.ds(pl.multiple_of(y * TILE, TILE), TILE), :]
    for d in range(2):
        for piece in (1, 2):
            p1_copy(d, piece).wait_recv()
        order = (2, 1) if d == 0 else (1, 2)
        total = total + jnp.concatenate([p1_in[d, piece] for piece in order], axis=0).astype(f32)
    finish(0, total)
    for part in range(2):
        total = p2[part, z]
        for slot in (3, 6):
            p2_copy(part, slot).wait_recv()
            total = total + p2_in[part, slot].astype(f32)
        finish(TILE + part * HALF, total)

    for copy in (
        right_low, left_high, right_high, left_low, own_across,
        on_right, on_left, before_across, after_across, opposite_across,
    ):
        copy.wait_send()
    for d in range(2):
        for s in (NZ - 3, NZ - 2):
            for u in range(2):
                z_copy(d, s, u).wait_send()
        for s in range(6):
            y_copy(d, s).wait_send()
    for part in range(2):
        for slot in range(7):
            p2_copy(part, slot).wait_send()
    for d in range(2):
        for piece in range(3):
            p1_copy(d, piece).wait_send()


def body(features, weight, bias, edge_src, edge_dst, tile_count):
    vmem = pl.BlockSpec(memory_space=pltpu.VMEM)
    smem = pl.BlockSpec(memory_space=pltpu.SMEM)
    units = features.shape[1]
    dma = pltpu.SemaphoreType.DMA
    return pl.pallas_call(
        kernel,
        out_shape=jax.ShapeDtypeStruct((2 * TILE, F), bf16),
        in_specs=[vmem, vmem, vmem, smem, vmem, vmem],
        out_specs=vmem,
        scratch_shapes=[
            pltpu.VMEM((NROW, units, SRC), bf16),
            pltpu.VMEM((F, SRC), bf16),
            pltpu.VMEM((32, 64), f32),
            pltpu.VMEM((NROW - 1, 32, 64), f32),
            pltpu.VMEM((NZ, 8, 128), f32),
            pltpu.VMEM((NZ - 1, 8, 128), f32),
            pltpu.VMEM((8, 128), f32),
            pltpu.VMEM((NY - 1, 8, 128), f32),
            pltpu.VMEM((TILES * TILE, SRC), bf16),
            pltpu.VMEM((2, 2, 2 * TILE, F), bf16),
            pltpu.VMEM((2, NZ - 1, 2 * TILE, F), bf16),
            pltpu.VMEM((2, 6, 2 * TILE, F), bf16),
            pltpu.VMEM((2, 6, 2 * TILE, F), bf16),
            pltpu.VMEM((2, 3, HALF, F), bf16),
            pltpu.VMEM((2, 3, HALF, F), bf16),
            pltpu.VMEM((2, NZ, HALF, F), f32),
            pltpu.VMEM((2, 7, HALF, F), bf16),
            pltpu.VMEM((2, 7, HALF, F), bf16),
            pltpu.VMEM((STEP, F), f32),
            pltpu.VMEM((STEP // 2, F), f32),
            dma((2, 10)),
            dma((2, NROW - 1)),
            dma((2, NZ - 1)),
            dma((2, NY - 1)),
            dma((2, 2, NZ - 1, 2)),
            dma((2, 2, 6)),
            dma((2, 2, 3)),
            dma((2, 2, 7)),
            dma,
        ],
        compiler_params=pltpu.CompilerParams(
            collective_id=0, has_side_effects=True, vmem_limit_bytes=60 * 1024 * 1024
        ),
        name="graph_layer",
    )(features.T, edge_src, edge_dst, tile_count.T, weight, bias[None, :])


def solution(mesh):
    in_specs = (P("col", "row"), P(), P(), P("row", "col"), P("row", "col"), P("row", "col"))
    out_specs = P(("row", "col"), None)
    return jax.shard_map(body, mesh=mesh, in_specs=in_specs, out_specs=out_specs, check_vma=False)
```

```python
import functools

import jax
import jax.numpy as jnp
from jax import lax
from jax.experimental import pallas as pl
from jax.experimental.pallas import tpu as pltpu
from jax.sharding import PartitionSpec as P

TILE = 128
F = 512
SRC = 2048
CAP = 512
TILES = 64
NROW = 8
NY = 4
NZ = 8
HALF = 64
AHEAD = 2
STEP = 1024
bf16 = jnp.bfloat16
f32 = jnp.float32
f8 = jnp.float8_e4m3fn
MESH = pl.DeviceIdType.MESH
NT = (((1,), (1,)), ((), ()))


def onehot(row, size):
    parts = []
    for base in range(0, size, 256):
        width = min(256, size - base)
        value = (row - base).astype(f32).astype(bf16)
        places = lax.broadcasted_iota(jnp.int32, (width, row.shape[1]), 0).astype(f32).astype(bf16)
        parts.append(jnp.where(places == value, jnp.ones((), bf16), jnp.zeros((), bf16)).astype(f8))
    return parts[0] if len(parts) == 1 else jnp.concatenate(parts, axis=0)


def kernel(
    xt, src, dst, cnt, weight, bias, out,
    xg, xs, deg, deg_in, cin, cin_in, cmid, cmid_in, amat,
    zs, zr, ys, yr, p1, p1_in, p2, p2_out, p2_in, acc, acc_y,
    x_sem, d_sem, c_sem, m_sem, z_sem, y_sem, p1_sem, p2_sem, own_sem,
):
    r = lax.axis_index("row")
    c = lax.axis_index("col")
    y = c // NZ
    z = lax.rem(c, NZ)

    def row_peer(k):
        return (lax.rem(r + k, NROW), c)

    def z_peer(k):
        return (r, y * NZ + lax.rem(z + k, NZ))

    def y_peer(k):
        return (r, lax.rem(y + k, NY) * NZ + z)

    barrier = pltpu.get_barrier_semaphore()
    peers = [row_peer(k) for k in range(1, NROW)]
    peers += [z_peer(k) for k in range(1, NZ)]
    peers += [y_peer(k) for k in range(1, NY)]
    for peer in peers:
        pl.semaphore_signal(barrier, inc=1, device_id=peer, device_id_type=MESH)
    pl.semaphore_wait(barrier, len(peers))

    def remote(source, target, sems, index, peer):
        return pltpu.make_async_remote_copy(
            src_ref=source, dst_ref=target, send_sem=sems.at[(0,) + index],
            recv_sem=sems.at[(1,) + index], device_id=peer, device_id_type=MESH,
        )

    after, before, opposite = (lax.rem(r + k, NROW) for k in (2, 6, 4))
    sibling = (r + 1 - 2 * lax.rem(r, 2), c)
    low, high = pl.ds(0, 32), pl.ds(32, 32)

    def x_copy(index, source, target, peer):
        return remote(source, target, x_sem, (index,), peer)

    right_low = x_copy(0, xt.at[low], xg.at[r, low], (after, c))
    left_high = x_copy(1, xt.at[high], xg.at[r, high], (before, c))
    right_high = x_copy(2, xt.at[high], xg.at[r, high], (after, c))
    left_low = x_copy(3, xt.at[low], xg.at[r, low], (before, c))
    own_across = x_copy(4, xt, xg.at[r], sibling)
    on_right = x_copy(5, xg.at[before, low], xg.at[before, low], (after, c))
    on_left = x_copy(6, xg.at[after, high], xg.at[after, high], (before, c))
    before_across = x_copy(7, xg.at[before], xg.at[before], sibling)
    after_across = x_copy(8, xg.at[after], xg.at[after], sibling)
    opposite_across = x_copy(9, xg.at[opposite], xg.at[opposite], sibling)
    for copy in (right_low, left_high, own_across):
        copy.start()
    own = pltpu.make_async_copy(xt, xg.at[r], own_sem)
    own.start()

    slots = lax.broadcasted_iota(jnp.int32, (1, CAP), 1)

    def edges(t):
        return src[pl.ds(t, 1), :], dst[pl.ds(t, 1), :], slots < cnt[0, t]

    def source_step(i, total):
        for j in range(8):
            s, _, valid = edges(i * 8 + j)
            left = onehot(jnp.where(valid, s >> 6, -1), 32)
            total = total + lax.dot_general(left, onehot(s & 63, 64), NT, preferred_element_type=f32)
        return total

    deg[...] = lax.fori_loop(0, TILES // 8, source_step, jnp.zeros((32, 64), f32))
    d_copies = [remote(deg, deg_in.at[k - 1], d_sem, (k - 1,), row_peer(k)) for k in range(1, NROW)]
    for copy in d_copies:
        copy.start()
    right_low.wait_recv()
    on_right.start()
    left_high.wait_recv()
    on_left.start()
    right_high.start()
    left_low.start()

    def target_step(zi):
        rows = []
        for j in range(8):
            _, d, valid = edges(2 * ((j // 2) * NZ + zi) + j % 2)
            right = onehot(jnp.where(valid, d, -1), 128)
            rows.append(
                lax.dot_general(jnp.ones((32, CAP), f8), right, NT, preferred_element_type=f32)[:1]
            )
        cin[zi] = jnp.concatenate(rows, axis=0)

    def target_steps(first):
        def one(i, carry):
            target_step(i)
            return carry

        lax.fori_loop(first, first + 4, one, 0)

    c_copies = [
        remote(cin.at[lax.rem(z + k, NZ)], cin_in.at[k - 1], c_sem, (k - 1,), z_peer(k))
        for k in range(1, NZ)
    ]
    m_copies = [remote(cmid, cmid_in.at[k - 1], m_sem, (k - 1,), y_peer(k)) for k in range(1, NY)]
    def count_matrix(t):
        s, d, valid = edges(t)
        place = jnp.where(valid, (s >> 9) * TILE + d, -1)
        return lax.dot_general(
            onehot(place, 512), onehot(s & 511, 512), NT, preferred_element_type=f32
        ).astype(bf16)

    def build(p):
        group = p // 2
        is_y = lax.rem(p, 2)
        q = group // 2
        d = lax.rem(group, 2)
        yi = lax.rem(y + 2 * NY + (2 * d - 1) * (q + 1), NY)
        for jj in range(4):
            zi = lax.rem(z + NZ - 1 - group, NZ) if jj < 2 else lax.rem(z + 1 + group, NZ)
            z_tile = 2 * (jj * NZ + zi)
            y_tile = 2 * (yi * NZ + 4 * d + jj) + 1
            count = count_matrix(z_tile + is_y * (y_tile - z_tile))
            z_base = group * STEP + jj * TILE
            y_base = 2 * q * STEP + 512 + d * 256 + jj * HALF
            base = z_base + is_y * (y_base - z_base)
            for part in range(2):
                first = pl.multiple_of(base + part * (HALF + is_y * (STEP - HALF)), HALF)
                for h in range(4):
                    start = h * TILE + part * HALF
                    amat[pl.ds(first, HALF), h * 512 : (h + 1) * 512] = count[start : start + HALF]

    def ahead(p, carry):
        @pl.when(p == 2)
        def _():
            right_high.wait_recv()
            before_across.start()
            left_low.wait_recv()
            after_across.start()

        @pl.when(p == 3)
        def _():
            on_right.wait_recv()
            on_left.wait_recv()
            opposite_across.start()

        build(p)
        return carry

    lax.fori_loop(0, 2 * AHEAD + 2, ahead, 0)
    target_steps(0)
    for copy in d_copies:
        copy.wait()
    total = deg[...]
    for k in range(1, NROW):
        total = total + deg_in[k - 1]
    scale = lax.rsqrt(1.0 + total)
    scale = [
        jnp.concatenate([scale[2 * h : 2 * h + 1], scale[2 * h + 1 : 2 * h + 2]], axis=1)
        for h in range(16)
    ]
    own.wait()

    def scale_rows(offset):
        def one(i, carry):
            piece = lax.rem(offset + 2 * i, NROW)
            base = pl.multiple_of(piece * 64, 64)
            for h in range(16):
                cols = slice(h * 128, (h + 1) * 128)
                xs[pl.ds(base, 64), cols] = (xg[piece, :, cols].astype(f32) * scale[h]).astype(bf16)
            return carry

        lax.fori_loop(0, 4, one, 0)

    scale_rows(r)
    for copy in (own_across, before_across, after_across, opposite_across):
        copy.wait_recv()
    scale_rows(r + 1)

    def product(first, rows, target):
        def one(i, carry):
            base = pl.multiple_of(first + i * 512, 512)
            target[pl.ds(pl.multiple_of(i * 512, 512), 512), :] = lax.dot_general(
                amat[pl.ds(base, 512), :], xs[...], NT, preferred_element_type=f32
            )
            return carry

        lax.fori_loop(0, rows // 512, one, 0)

    def z_copy(d, s, u):
        rows = pl.ds(u * TILE, TILE)
        return remote(
            zs.at[d, lax.rem(s, 2), rows], zr.at[d, s, rows], z_sem, (d, s, u),
            z_peer(1 if d == 0 else NZ - 1),
        )

    def y_copy(d, s):
        return remote(ys.at[d, s], yr.at[d, s], y_sem, (d, s), y_peer(1 if d == 0 else NY - 1))

    def z_sum(d, s, u):
        z_copy(d, s - 1, u).wait_recv()
        rows = slice(d * 256 + u * TILE, d * 256 + (u + 1) * TILE)
        return acc[rows] + zr[d, s - 1, u * TILE : (u + 1) * TILE].astype(f32)

    def z_add(d, s, u):
        acc[d * 256 + u * TILE : d * 256 + (u + 1) * TILE] = z_sum(d, s, u)

    def z_send(d, s, u, value):
        zs[d, lax.rem(s, 2), u * TILE : (u + 1) * TILE] = value.astype(bf16)
        z_copy(d, s, u).start()

    def z_part(d, s, u):
        value = z_sum(d, s, u)

        @pl.when(s > 1)
        def _():
            z_copy(d, s - 2, u).wait_send()

        z_send(d, s, u, value)

    def y_first(d, s):
        ys[d, s] = acc[512 + d * 256 : 768 + d * 256].astype(bf16)
        y_copy(d, s).start()

    def y_part(d, s):
        y_copy(d, s - 2).wait_recv()
        value = acc[512 + d * 256 : 768 + d * 256] + yr[d, s - 2].astype(f32)
        ys[d, s] = value.astype(bf16)
        y_copy(d, s).start()

    def y_last(part, source, offset):
        for d in range(2):
            y_copy(d, 4 + part).wait_recv()
            for u in range(4):
                first = offset + d * 256 + u * HALF
                p2[part, 4 * d + u] = source[first : first + HALF] + yr[
                    d, 4 + part, u * HALF : (u + 1) * HALF
                ].astype(f32)

    def p2_copy(part, slot):
        return remote(
            p2_out.at[part, slot], p2_in.at[part, slot], p2_sem, (part, slot),
            z_peer(1 if slot < 4 else NZ - 1),
        )

    def p2_hop(part, hop):
        for slot in (hop, 4 + hop) if hop < 3 else (hop,):
            zi = lax.rem(z + (4 - hop if slot < 4 else 5 + hop), NZ)
            value = p2[part, zi]
            if hop > 0:
                p2_copy(part, slot - 1).wait_recv()
                value = value + p2_in[part, slot - 1].astype(f32)
            p2_out[part, slot] = value.astype(bf16)
            p2_copy(part, slot).start()

    def ring_step(s, carry):
        sends = s > 0

        @pl.when(jnp.logical_and(s > 0, s < NZ - AHEAD))
        def _():
            def one(p, carry):
                build(p)
                return carry

            lax.fori_loop(2 * (s + AHEAD), 2 * (s + AHEAD) + 2, one, 0)

        product(s * STEP, STEP, acc)

        @pl.when(s == 0)
        def _():
            for u in range(2):
                for d in range(2):
                    z_send(d, s, u, acc[d * 256 + u * TILE : d * 256 + (u + 1) * TILE])

        @pl.when(sends)
        def _():
            for d in range(2):
                z_part(d, s, 0)

        @pl.when(s < 2)
        def _():
            for d in range(2):
                y_first(d, s)

        @pl.when(jnp.logical_and(s > 1, s < 6))
        def _():
            for d in range(2):
                y_part(d, s)

        @pl.when(s == 6)
        def _():
            y_last(0, acc, 512)
            p2_hop(0, 0)
            product((NZ - 1) * STEP + 512, 512, acc_y)

        @pl.when(sends)
        def _():
            for d in range(2):
                z_part(d, s, 1)

        @pl.when(s == 0)
        def _():
            target_steps(4)
            for copy in c_copies:
                copy.start()

        @pl.when(s == 3)
        def _():
            for copy in c_copies:
                copy.wait()
            mid = cin[z]
            for k in range(1, NZ):
                mid = mid + cin_in[k - 1]
            cmid[...] = mid
            for copy in m_copies:
                copy.start()

        return carry

    lax.fori_loop(0, NZ - 1, ring_step, 0)
    y_last(1, acc_y, 0)
    p2_hop(1, 0)
    p2_hop(0, 1)
    product((NZ - 1) * STEP, 512, acc)
    for d in range(2):
        z_add(d, NZ - 1, 0)
    p2_hop(0, 2)
    p2_hop(1, 1)
    for d in range(2):
        z_add(d, NZ - 1, 1)

    def p1_copy(d, piece):
        return remote(
            p1.at[d, piece], p1_in.at[d, piece], p1_sem, (d, piece), y_peer(1 if d == 0 else NY - 1)
        )

    def p1_send(d, piece):
        yi = lax.rem(y + (2 if piece == 0 else 1 if d == 0 else 3), NY)
        half = d if piece in (0, 2) else 1 - d
        value = acc[pl.ds(pl.multiple_of(yi * TILE + half * HALF, HALF), HALF), :]
        if piece == 2:
            p1_copy(d, 0).wait_recv()
            value = value + p1_in[d, 0].astype(f32)
        p1[d, piece] = value.astype(bf16)
        p1_copy(d, piece).start()

    for piece in range(2):
        for d in range(2):
            p1_send(d, piece)
    p2_hop(0, 3)
    p2_hop(1, 2)
    for d in range(2):
        p1_send(d, 2)
    for copy in (
        right_low, left_high, right_high, left_low, own_across,
        on_right, on_left, before_across, after_across, opposite_across,
    ):
        copy.wait_send()
    for d in range(2):
        for s in (NZ - 3, NZ - 2):
            for u in range(2):
                z_copy(d, s, u).wait_send()
        for s in range(6):
            y_copy(d, s).wait_send()
    for copy in m_copies:
        copy.wait()
    degree = cmid[pl.ds(2 * y, 2), :]
    for k in range(1, NY):
        degree = degree + cmid_in[k - 1, pl.ds(2 * y, 2), :]
    norm = jnp.transpose(lax.rsqrt(1.0 + jnp.concatenate([degree] * 4, axis=0)))

    p2_hop(1, 3)

    def finish(first, total):
        rows = total.shape[0]
        half, start = first // TILE, first % TILE
        normed = (total * norm[start : start + rows, half : half + 1]).astype(bf16)
        result = jnp.dot(normed, weight[...], preferred_element_type=f32) + bias[...]
        out[first : first + rows, :] = jnp.maximum(result, 0.0).astype(bf16)

    total = acc[pl.ds(pl.multiple_of(y * TILE, TILE), TILE), :]
    for d in range(2):
        for piece in (1, 2):
            p1_copy(d, piece).wait_recv()
        order = (2, 1) if d == 0 else (1, 2)
        total = total + jnp.concatenate([p1_in[d, piece] for piece in order], axis=0).astype(f32)
    finish(0, total)
    for part in range(2):
        total = p2[part, z]
        for slot in (3, 6):
            p2_copy(part, slot).wait_recv()
            total = total + p2_in[part, slot].astype(f32)
        finish(TILE + part * HALF, total)

    for part in range(2):
        for slot in range(7):
            p2_copy(part, slot).wait_send()
    for d in range(2):
        for piece in range(3):
            p1_copy(d, piece).wait_send()


def body(features, weight, bias, edge_src, edge_dst, tile_count):
    vmem = pl.BlockSpec(memory_space=pltpu.VMEM)
    smem = pl.BlockSpec(memory_space=pltpu.SMEM)
    units = features.shape[1]
    dma = pltpu.SemaphoreType.DMA
    return pl.pallas_call(
        kernel,
        out_shape=jax.ShapeDtypeStruct((2 * TILE, F), bf16),
        in_specs=[vmem, vmem, vmem, smem, vmem, vmem],
        out_specs=vmem,
        scratch_shapes=[
            pltpu.VMEM((NROW, units, SRC), bf16),
            pltpu.VMEM((F, SRC), bf16),
            pltpu.VMEM((32, 64), f32),
            pltpu.VMEM((NROW - 1, 32, 64), f32),
            pltpu.VMEM((NZ, 8, 128), f32),
            pltpu.VMEM((NZ - 1, 8, 128), f32),
            pltpu.VMEM((8, 128), f32),
            pltpu.VMEM((NY - 1, 8, 128), f32),
            pltpu.VMEM((TILES * TILE, SRC), bf16),
            pltpu.VMEM((2, 2, 2 * TILE, F), bf16),
            pltpu.VMEM((2, NZ - 1, 2 * TILE, F), bf16),
            pltpu.VMEM((2, 6, 2 * TILE, F), bf16),
            pltpu.VMEM((2, 6, 2 * TILE, F), bf16),
            pltpu.VMEM((2, 3, HALF, F), bf16),
            pltpu.VMEM((2, 3, HALF, F), bf16),
            pltpu.VMEM((2, NZ, HALF, F), f32),
            pltpu.VMEM((2, 7, HALF, F), bf16),
            pltpu.VMEM((2, 7, HALF, F), bf16),
            pltpu.VMEM((STEP, F), f32),
            pltpu.VMEM((STEP // 2, F), f32),
            dma((2, 10)),
            dma((2, NROW - 1)),
            dma((2, NZ - 1)),
            dma((2, NY - 1)),
            dma((2, 2, NZ - 1, 2)),
            dma((2, 2, 6)),
            dma((2, 2, 3)),
            dma((2, 2, 7)),
            dma,
        ],
        compiler_params=pltpu.CompilerParams(
            collective_id=0, has_side_effects=True, vmem_limit_bytes=60 * 1024 * 1024
        ),
        name="graph_layer",
    )(features.T, edge_src, edge_dst, tile_count.T, weight, bias[None, :])


def solution(mesh):
    in_specs = (P("col", "row"), P(), P(), P("row", "col"), P("row", "col"), P("row", "col"))
    out_specs = P(("row", "col"), None)
    return jax.shard_map(body, mesh=mesh, in_specs=in_specs, out_specs=out_specs, check_vma=False)
```

```python
import functools

import jax
import jax.numpy as jnp
from jax import lax
from jax.experimental import pallas as pl
from jax.experimental.pallas import tpu as pltpu
from jax.sharding import PartitionSpec as P

TILE = 128
F = 512
SRC = 2048
CAP = 512
TILES = 64
NROW = 8
NY = 4
NZ = 8
HALF = 64
AHEAD = 2
STEP = 1024
bf16 = jnp.bfloat16
f32 = jnp.float32
f8 = jnp.float8_e4m3fn
MESH = pl.DeviceIdType.MESH
NT = (((1,), (1,)), ((), ()))


def onehot(row, size):
    parts = []
    for base in range(0, size, 256):
        width = min(256, size - base)
        value = (row - base).astype(f32).astype(bf16)
        places = lax.broadcasted_iota(jnp.int32, (width, row.shape[1]), 0).astype(f32).astype(bf16)
        parts.append(jnp.where(places == value, jnp.ones((), bf16), jnp.zeros((), bf16)).astype(f8))
    return parts[0] if len(parts) == 1 else jnp.concatenate(parts, axis=0)


def kernel(
    xt, src, dst, cnt, weight, bias, out,
    xg, xs, deg, deg_in, cin, cin_in, cmid, cmid_in, amat,
    zs, zr, ys, yr, p1, p1_in, p2, p2_out, p2_in, acc, acc_y,
    x_sem, d_sem, c_sem, m_sem, z_sem, y_sem, p1_sem, p2_sem, own_sem,
):
    r = lax.axis_index("row")
    c = lax.axis_index("col")
    y = c // NZ
    z = lax.rem(c, NZ)

    def row_peer(k):
        return (lax.rem(r + k, NROW), c)

    def z_peer(k):
        return (r, y * NZ + lax.rem(z + k, NZ))

    def y_peer(k):
        return (r, lax.rem(y + k, NY) * NZ + z)

    barrier = pltpu.get_barrier_semaphore()
    peers = [row_peer(k) for k in range(1, NROW)]
    peers += [z_peer(k) for k in range(1, NZ)]
    peers += [y_peer(k) for k in range(1, NY)]
    for peer in peers:
        pl.semaphore_signal(barrier, inc=1, device_id=peer, device_id_type=MESH)
    pl.semaphore_wait(barrier, len(peers))

    def remote(source, target, sems, index, peer):
        return pltpu.make_async_remote_copy(
            src_ref=source, dst_ref=target, send_sem=sems.at[(0,) + index],
            recv_sem=sems.at[(1,) + index], device_id=peer, device_id_type=MESH,
        )

    after, before, opposite = (lax.rem(r + k, NROW) for k in (2, 6, 4))
    sibling = (r + 1 - 2 * lax.rem(r, 2), c)
    low, high = pl.ds(0, 32), pl.ds(32, 32)

    def x_copy(index, source, target, peer):
        return remote(source, target, x_sem, (index,), peer)

    right_low = x_copy(0, xt.at[low], xg.at[r, low], (after, c))
    left_high = x_copy(1, xt.at[high], xg.at[r, high], (before, c))
    right_high = x_copy(2, xt.at[high], xg.at[r, high], (after, c))
    left_low = x_copy(3, xt.at[low], xg.at[r, low], (before, c))
    own_across = x_copy(4, xt, xg.at[r], sibling)
    on_right = x_copy(5, xg.at[before, low], xg.at[before, low], (after, c))
    on_left = x_copy(6, xg.at[after, high], xg.at[after, high], (before, c))
    before_across = x_copy(7, xg.at[before], xg.at[before], sibling)
    after_across = x_copy(8, xg.at[after], xg.at[after], sibling)
    opposite_across = x_copy(9, xg.at[opposite], xg.at[opposite], sibling)
    for copy in (right_low, left_high, own_across):
        copy.start()
    own = pltpu.make_async_copy(xt, xg.at[r], own_sem)
    own.start()

    slots = lax.broadcasted_iota(jnp.int32, (1, CAP), 1)

    def edges(t):
        return src[pl.ds(t, 1), :], dst[pl.ds(t, 1), :], slots < cnt[0, t]

    def source_step(i, total):
        for j in range(8):
            s, _, valid = edges(i * 8 + j)
            left = onehot(jnp.where(valid, s >> 6, -1), 32)
            total = total + lax.dot_general(left, onehot(s & 63, 64), NT, preferred_element_type=f32)
        return total

    deg[...] = lax.fori_loop(0, TILES // 8, source_step, jnp.zeros((32, 64), f32))
    d_copies = [remote(deg, deg_in.at[k - 1], d_sem, (k - 1,), row_peer(k)) for k in range(1, NROW)]
    for copy in d_copies:
        copy.start()
    right_low.wait_recv()
    on_right.start()
    left_high.wait_recv()
    on_left.start()
    right_high.start()
    left_low.start()

    def target_step(zi):
        rows = []
        for j in range(8):
            _, d, valid = edges(2 * ((j // 2) * NZ + zi) + j % 2)
            right = onehot(jnp.where(valid, d, -1), 128)
            rows.append(
                lax.dot_general(jnp.ones((32, CAP), f8), right, NT, preferred_element_type=f32)[:1]
            )
        cin[zi] = jnp.concatenate(rows, axis=0)

    def target_steps(first):
        def one(i, carry):
            target_step(i)
            return carry

        lax.fori_loop(first, first + 4, one, 0)

    c_copies = [
        remote(cin.at[lax.rem(z + k, NZ)], cin_in.at[k - 1], c_sem, (k - 1,), z_peer(k))
        for k in range(1, NZ)
    ]
    m_copies = [remote(cmid, cmid_in.at[k - 1], m_sem, (k - 1,), y_peer(k)) for k in range(1, NY)]
    def count_matrix(t):
        s, d, valid = edges(t)
        place = jnp.where(valid, (s >> 9) * TILE + d, -1)
        return lax.dot_general(
            onehot(place, 512), onehot(s & 511, 512), NT, preferred_element_type=f32
        ).astype(bf16)

    def build(p):
        group = p // 2
        is_y = lax.rem(p, 2)
        q = group // 2
        d = lax.rem(group, 2)
        yi = lax.rem(y + 2 * NY + (2 * d - 1) * (q + 1), NY)
        for jj in range(4):
            zi = lax.rem(z + NZ - 1 - group, NZ) if jj < 2 else lax.rem(z + 1 + group, NZ)
            z_tile = 2 * (jj * NZ + zi)
            y_tile = 2 * (yi * NZ + 4 * d + jj) + 1
            count = count_matrix(z_tile + is_y * (y_tile - z_tile))
            z_base = group * STEP + jj * TILE
            y_base = 2 * q * STEP + 512 + d * 256 + jj * HALF
            base = z_base + is_y * (y_base - z_base)
            for part in range(2):
                first = pl.multiple_of(base + part * (HALF + is_y * (STEP - HALF)), HALF)
                for h in range(4):
                    start = h * TILE + part * HALF
                    amat[pl.ds(first, HALF), h * 512 : (h + 1) * 512] = count[start : start + HALF]

    def ahead(p, carry):
        @pl.when(p == 2)
        def _():
            right_high.wait_recv()
            before_across.start()
            left_low.wait_recv()
            after_across.start()

        @pl.when(p == 3)
        def _():
            on_right.wait_recv()
            on_left.wait_recv()
            opposite_across.start()

        build(p)
        return carry

    lax.fori_loop(0, 2 * AHEAD + 2, ahead, 0)
    target_steps(0)
    for copy in d_copies:
        copy.wait()
    total = deg[...]
    for k in range(1, NROW):
        total = total + deg_in[k - 1]
    scale = lax.rsqrt(1.0 + total)
    scale = [
        jnp.concatenate([scale[2 * h : 2 * h + 1], scale[2 * h + 1 : 2 * h + 2]], axis=1)
        for h in range(16)
    ]
    own.wait()

    def scale_rows(offset):
        def one(i, carry):
            piece = lax.rem(offset + 2 * i, NROW)
            base = pl.multiple_of(piece * 64, 64)
            for h in range(16):
                cols = slice(h * 128, (h + 1) * 128)
                xs[pl.ds(base, 64), cols] = (xg[piece, :, cols].astype(f32) * scale[h]).astype(bf16)
            return carry

        lax.fori_loop(0, 4, one, 0)

    scale_rows(r)
    for copy in (own_across, before_across, after_across, opposite_across):
        copy.wait_recv()
    scale_rows(r + 1)

    def product(first, rows, target):
        def one(i, carry):
            base = pl.multiple_of(first + i * 512, 512)
            target[pl.ds(pl.multiple_of(i * 512, 512), 512), :] = lax.dot_general(
                amat[pl.ds(base, 512), :], xs[...], NT, preferred_element_type=f32
            )
            return carry

        lax.fori_loop(0, rows // 512, one, 0)

    def z_copy(d, s, u):
        rows = pl.ds(u * TILE, TILE)
        return remote(
            zs.at[d, lax.rem(s, 2), rows], zr.at[d, s, rows], z_sem, (d, s, u),
            z_peer(1 if d == 0 else NZ - 1),
        )

    def y_copy(d, s):
        return remote(ys.at[d, s], yr.at[d, s], y_sem, (d, s), y_peer(1 if d == 0 else NY - 1))

    def z_sum(d, s, u):
        z_copy(d, s - 1, u).wait_recv()
        rows = slice(d * 256 + u * TILE, d * 256 + (u + 1) * TILE)
        return acc[rows] + zr[d, s - 1, u * TILE : (u + 1) * TILE].astype(f32)

    def z_add(d, s, u):
        acc[d * 256 + u * TILE : d * 256 + (u + 1) * TILE] = z_sum(d, s, u)

    def z_send(d, s, u, value):
        zs[d, lax.rem(s, 2), u * TILE : (u + 1) * TILE] = value.astype(bf16)
        z_copy(d, s, u).start()

    def z_part(d, s, u):
        value = z_sum(d, s, u)

        @pl.when(s > 1)
        def _():
            z_copy(d, s - 2, u).wait_send()

        z_send(d, s, u, value)

    def y_first(d, s):
        ys[d, s] = acc[512 + d * 256 : 768 + d * 256].astype(bf16)
        y_copy(d, s).start()

    def y_part(d, s):
        y_copy(d, s - 2).wait_recv()
        value = acc[512 + d * 256 : 768 + d * 256] + yr[d, s - 2].astype(f32)
        ys[d, s] = value.astype(bf16)
        y_copy(d, s).start()

    def y_last(part, source, offset):
        for d in range(2):
            y_copy(d, 4 + part).wait_recv()
            for u in range(4):
                first = offset + d * 256 + u * HALF
                p2[part, 4 * d + u] = source[first : first + HALF] + yr[
                    d, 4 + part, u * HALF : (u + 1) * HALF
                ].astype(f32)

    def p2_copy(part, slot):
        return remote(
            p2_out.at[part, slot], p2_in.at[part, slot], p2_sem, (part, slot),
            z_peer(1 if slot < 4 else NZ - 1),
        )

    def p2_hop(part, hop):
        for slot in (hop, 4 + hop) if hop < 3 else (hop,):
            zi = lax.rem(z + (4 - hop if slot < 4 else 5 + hop), NZ)
            value = p2[part, zi]
            if hop > 0:
                p2_copy(part, slot - 1).wait_recv()
                value = value + p2_in[part, slot - 1].astype(f32)
            p2_out[part, slot] = value.astype(bf16)
            p2_copy(part, slot).start()

    def ring_step(s, carry):
        sends = s > 0

        @pl.when(jnp.logical_and(s > 0, s < NZ - AHEAD))
        def _():
            def one(p, carry):
                build(p)
                return carry

            lax.fori_loop(2 * (s + AHEAD), 2 * (s + AHEAD) + 2, one, 0)

        @pl.when(s == NZ - 2)
        def _():
            target_steps(4)
            for copy in c_copies:
                copy.start()

        product(s * STEP, STEP, acc)

        @pl.when(s < 2)
        def _():
            for d in range(2):
                y_first(d, s)

        @pl.when(jnp.logical_and(s > 1, s < 6))
        def _():
            for d in range(2):
                y_part(d, s)

        @pl.when(s == 0)
        def _():
            for u in range(2):
                for d in range(2):
                    z_send(d, s, u, acc[d * 256 + u * TILE : d * 256 + (u + 1) * TILE])

        @pl.when(sends)
        def _():
            for d in range(2):
                z_part(d, s, 0)

        @pl.when(s == 6)
        def _():
            y_last(0, acc, 512)
            p2_hop(0, 0)
            product((NZ - 1) * STEP + 512, 512, acc_y)

        @pl.when(sends)
        def _():
            for d in range(2):
                z_part(d, s, 1)

        return carry

    lax.fori_loop(0, NZ - 1, ring_step, 0)
    y_last(1, acc_y, 0)
    p2_hop(1, 0)
    p2_hop(0, 1)
    product((NZ - 1) * STEP, 512, acc)
    for copy in c_copies:
        copy.wait()
    mid = cin[z]
    for k in range(1, NZ):
        mid = mid + cin_in[k - 1]
    cmid[...] = mid
    for copy in m_copies:
        copy.start()
    for d in range(2):
        z_add(d, NZ - 1, 0)
    p2_hop(0, 2)
    p2_hop(1, 1)
    for d in range(2):
        z_add(d, NZ - 1, 1)

    def p1_copy(d, piece):
        return remote(
            p1.at[d, piece], p1_in.at[d, piece], p1_sem, (d, piece), y_peer(1 if d == 0 else NY - 1)
        )

    def p1_send(d, piece):
        yi = lax.rem(y + (2 if piece == 0 else 1 if d == 0 else 3), NY)
        half = d if piece in (0, 2) else 1 - d
        value = acc[pl.ds(pl.multiple_of(yi * TILE + half * HALF, HALF), HALF), :]
        if piece == 2:
            p1_copy(d, 0).wait_recv()
            value = value + p1_in[d, 0].astype(f32)
        p1[d, piece] = value.astype(bf16)
        p1_copy(d, piece).start()

    for piece in range(2):
        for d in range(2):
            p1_send(d, piece)
    p2_hop(0, 3)
    p2_hop(1, 2)
    for d in range(2):
        p1_send(d, 2)
    p2_hop(1, 3)

    for copy in m_copies:
        copy.wait()
    degree = cmid[pl.ds(2 * y, 2), :]
    for k in range(1, NY):
        degree = degree + cmid_in[k - 1, pl.ds(2 * y, 2), :]
    norm = jnp.transpose(lax.rsqrt(1.0 + jnp.concatenate([degree] * 4, axis=0)))

    def finish(first, total):
        rows = total.shape[0]
        half, start = first // TILE, first % TILE
        normed = (total * norm[start : start + rows, half : half + 1]).astype(bf16)
        result = jnp.dot(normed, weight[...], preferred_element_type=f32) + bias[...]
        out[first : first + rows, :] = jnp.maximum(result, 0.0).astype(bf16)

    total = acc[pl.ds(pl.multiple_of(y * TILE, TILE), TILE), :]
    for d in range(2):
        for piece in (1, 2):
            p1_copy(d, piece).wait_recv()
        order = (2, 1) if d == 0 else (1, 2)
        total = total + jnp.concatenate([p1_in[d, piece] for piece in order], axis=0).astype(f32)
    finish(0, total)
    for part in range(2):
        total = p2[part, z]
        for slot in (3, 6):
            p2_copy(part, slot).wait_recv()
            total = total + p2_in[part, slot].astype(f32)
        finish(TILE + part * HALF, total)

    for copy in (
        right_low, left_high, right_high, left_low, own_across,
        on_right, on_left, before_across, after_across, opposite_across,
    ):
        copy.wait_send()
    for d in range(2):
        for s in (NZ - 3, NZ - 2):
            for u in range(2):
                z_copy(d, s, u).wait_send()
        for s in range(6):
            y_copy(d, s).wait_send()
    for part in range(2):
        for slot in range(7):
            p2_copy(part, slot).wait_send()
    for d in range(2):
        for piece in range(3):
            p1_copy(d, piece).wait_send()


def body(features, weight, bias, edge_src, edge_dst, tile_count):
    vmem = pl.BlockSpec(memory_space=pltpu.VMEM)
    smem = pl.BlockSpec(memory_space=pltpu.SMEM)
    units = features.shape[1]
    dma = pltpu.SemaphoreType.DMA
    return pl.pallas_call(
        kernel,
        out_shape=jax.ShapeDtypeStruct((2 * TILE, F), bf16),
        in_specs=[vmem, vmem, vmem, smem, vmem, vmem],
        out_specs=vmem,
        scratch_shapes=[
            pltpu.VMEM((NROW, units, SRC), bf16),
            pltpu.VMEM((F, SRC), bf16),
            pltpu.VMEM((32, 64), f32),
            pltpu.VMEM((NROW - 1, 32, 64), f32),
            pltpu.VMEM((NZ, 8, 128), f32),
            pltpu.VMEM((NZ - 1, 8, 128), f32),
            pltpu.VMEM((8, 128), f32),
            pltpu.VMEM((NY - 1, 8, 128), f32),
            pltpu.VMEM((TILES * TILE, SRC), bf16),
            pltpu.VMEM((2, 2, 2 * TILE, F), bf16),
            pltpu.VMEM((2, NZ - 1, 2 * TILE, F), bf16),
            pltpu.VMEM((2, 6, 2 * TILE, F), bf16),
            pltpu.VMEM((2, 6, 2 * TILE, F), bf16),
            pltpu.VMEM((2, 3, HALF, F), bf16),
            pltpu.VMEM((2, 3, HALF, F), bf16),
            pltpu.VMEM((2, NZ, HALF, F), f32),
            pltpu.VMEM((2, 7, HALF, F), bf16),
            pltpu.VMEM((2, 7, HALF, F), bf16),
            pltpu.VMEM((STEP, F), f32),
            pltpu.VMEM((STEP // 2, F), f32),
            dma((2, 10)),
            dma((2, NROW - 1)),
            dma((2, NZ - 1)),
            dma((2, NY - 1)),
            dma((2, 2, NZ - 1, 2)),
            dma((2, 2, 6)),
            dma((2, 2, 3)),
            dma((2, 2, 7)),
            dma,
        ],
        compiler_params=pltpu.CompilerParams(
            collective_id=0, has_side_effects=True, vmem_limit_bytes=60 * 1024 * 1024
        ),
        name="graph_layer",
    )(features.T, edge_src, edge_dst, tile_count.T, weight, bias[None, :])


def solution(mesh):
    in_specs = (P("col", "row"), P(), P(), P("row", "col"), P("row", "col"), P("row", "col"))
    out_specs = P(("row", "col"), None)
    return jax.shard_map(body, mesh=mesh, in_specs=in_specs, out_specs=out_specs, check_vma=False)
```
